256 devices in a mesh: ctx: 32 (over y, z), head: 8 (over x, core).
Axes of the slice: x: 4, y: 4, z: 8, core: 2. Of those that a mesh axis runs over, the one named last changes fastest.
Arguments:
- queries: bfloat16 [16384, 1024], P('ctx', 'head'), may hold values from -6 to 6
- keys: bfloat16 [16384, 1024], P('ctx', 'head'), may hold values from -6 to 6
- values: bfloat16 [16384, 1024], P('ctx', 'head'), may hold values from -6 to 6
- gain: float32 [1024], P('head'), may hold values from 0.1 to 1.9
- out_weight: bfloat16 [1024, 1024], P('head'), may hold values from -0.25 to 0.25
Outputs:
- mixed: bfloat16 [16384, 1024], P('ctx', 'head')
The draws below stay inside these ranges and needn't reach their ends.
All inputs are finite; a program needn't handle non-finite values.
Results may differ from the reference program's by a relative error of at most 0.0065.
Values may be sent and summed in bfloat16 or wider, within the bound.
A program may use at most 128 MiB of HBM per device.

```python
import jax
import jax.numpy as jnp
import numpy as np
from jax import lax

DH = 64
GROUP = 128
TOK_DEV = 512
HEADS = 16
D = 1024
TOKENS = 16384
N_CTX = 32


def with_spikes(drawn, rng, source, target, blocks, factor):
    def block_of(axis_at):
        return (jnp.arange(drawn.shape[axis_at]) // (drawn.shape[axis_at] // blocks)).reshape((-1,) + (1,) * (drawn.ndim - 1 - axis_at))

    near = jax.random.permutation(rng, blocks)[block_of(target)]
    far = (block_of(target) + blocks // 2) % blocks
    return jnp.where((block_of(source) == near) | (block_of(source) == far), factor * drawn, drawn)


def block_levels(own_key, extent, cuts, least, largest):
    factor_of, own = 1.0, jax.random.fold_in(own_key, 6)
    for dim, shards_of in cuts:
        heights = jnp.exp(jax.random.uniform(jax.random.fold_in(own, dim), (shards_of,), jnp.float32, least / len(cuts), largest / len(cuts)))
        factor_of = factor_of * jnp.repeat(heights, extent[dim] // shards_of).reshape([-1 if axis == dim else 1 for axis in range(len(extent))])
    return factor_of


def normal_values(key, shape, scale, most, cuts=(), kind=jnp.bfloat16):
    values = scale * jax.random.normal(key, shape, jnp.float32)
    if cuts:
        values = values * block_levels(key, shape, cuts, -0.22, 0.18)
    return jnp.clip(values, -most, most).astype(kind)


def gaussian_with(own_key, extent, deviation, bound, shards, heavy, held_as=jnp.bfloat16):
    entries = deviation * jax.random.normal(own_key, extent, jnp.float32)
    if shards:
        entries = entries * block_levels(own_key, extent, shards, -0.22, 0.18)
    return jnp.clip(with_spikes(entries, jax.random.fold_in(own_key, 3), *heavy), -bound, bound).astype(held_as)


def setup_inputs(seed: int = 0) -> dict:
    splits = jax.random.split(jax.random.key(seed), 6)
    return {
        "queries": normal_values(splits[0], (TOKENS, D), 1.0, 6.0, ((0, 32), (1, 8))),
        "keys": normal_values(splits[1], (TOKENS, D), 1.0, 6.0, ((0, 32), (1, 8))),
        "values": normal_values(splits[2], (TOKENS, D), 1.0, 6.0, ((0, 32), (1, 8))),
        "gain": jnp.clip(1.0 + 0.18 * jax.random.normal(splits[3], (D,), jnp.float32), 0.1, 1.9),
        "out_weight": gaussian_with(splits[4], (D, D), D ** -0.5, 0.25, ((0, 8),), (0, 1, 8, 2.0)),
    }


EPSILON = 1e-06

def expand(rows, doubled):
    width = rows.shape[-2]
    pieces = []
    for first in range(width):
        product = rows[..., first:first + 1, :] * rows[..., first:, :]
        if doubled:
            factor = np.where(np.arange(width - first) == 0, 1.0, 2.0).astype(np.float32)
            product = product * factor[:, None]
        pieces.append(product)
    return jnp.concatenate(pieces, axis=-2)

def rounded(array):
    return lax.optimization_barrier(array.astype(jnp.bfloat16)).astype(jnp.float32)

def reference(queries, keys, values, gain, out_weight):
    heads = HEADS
    feat = DH * (DH + 1) // 2
    groups = TOK_DEV // GROUP
    scaled = queries * 0.125
    shape = (N_CTX, groups, GROUP, heads, DH)
    query_blocks = scaled.reshape(shape)
    key_blocks = keys.reshape(shape)
    value_blocks = values.reshape(shape)
    causal = jnp.arange(GROUP)[:, None] >= jnp.arange(GROUP)[None, :]

    def slab_step(prefix, inputs):
        slab_rounded = rounded(prefix)

        def group_step(within, parts):
            query_part, key_part, value_part = parts
            query_feat = rounded(expand(jnp.transpose(query_part.astype(jnp.float32), (1, 2, 0)), True))
            key_feat = rounded(expand(jnp.transpose(key_part.astype(jnp.float32), (1, 2, 0)), False))
            values32 = value_part.astype(jnp.float32)
            inter = jnp.einsum('hft,hfd->thd', query_feat, slab_rounded)
            inter = inter + jnp.einsum('hft,hfd->thd', query_feat, rounded(within))
            scores = jnp.einsum('thd,shd->hts', query_part.astype(jnp.float32), key_part.astype(jnp.float32))
            weights = rounded(jnp.where(causal[None], scores * scores, 0.0))
            intra = jnp.einsum('hts,shd->thd', weights, values32)
            state = jnp.einsum('hft,thd->hfd', key_feat, values32)
            return (within + state, inter + intra)
        start = jnp.zeros((heads, feat, DH), jnp.float32)
        within, numer = lax.scan(group_step, start, inputs)
        return (prefix + within, numer)
    begin = jnp.zeros((heads, feat, DH), jnp.float32)
    numerator = lax.scan(slab_step, begin, (query_blocks, key_blocks, value_blocks))[1]
    numerator = numerator.reshape(TOKENS, heads, DH)
    meansq = lax.optimization_barrier(jnp.mean(numerator * numerator, axis=-1, keepdims=True))
    normed = numerator / jnp.sqrt(meansq + EPSILON) * gain.reshape(heads, DH)
    normed = normed.astype(jnp.bfloat16).reshape(TOKENS, D)
    return jnp.dot(normed, out_weight, preferred_element_type=jnp.float32).astype(jnp.bfloat16)
```

```python
import functools

import jax
import jax.numpy as jnp
from jax import lax
from jax.experimental import pallas as pl
from jax.experimental.pallas import tpu as pltpu
from jax.sharding import PartitionSpec as P

MESH = pl.DeviceIdType.MESH
DH = 64
LANES = 128
EPSILON = 1e-06
NZ = 8
NY = 4
NH = 8
ROUNDS = 4
EXTRA = 16
F32 = jnp.float32
BF16 = jnp.bfloat16


def nt(a, b):
    return lax.dot_general(a, b, (((1,), (1,)), ((), ())), preferred_element_type=F32)


def nn(a, b):
    return lax.dot_general(a, b, (((1,), (0,)), ((), ())), preferred_element_type=F32)


def rows_of(r):
    return DH + EXTRA if r == 0 else DH


def kernel(q_ref, k_ref, v_ref, gain_ref, w_ref, out_ref,
           kx, kz, qx, qz, vt, qf, num, wbuf, wt, ncat, send1, recv1, ybuf, send2, recv2,
           s1_send, s1_recv, y_send, y_recv, s2_send, s2_recv, w_send, w_recv, n_send, n_recv):
    ctx = lax.axis_index("ctx")
    y, z = ctx // NZ, lax.rem(ctx, NZ)
    me = lax.axis_index("head")
    tok = q_ref.shape[0]

    barrier = pltpu.get_barrier_semaphore()

    def greet(kind, count):
        def body(i, c):
            pl.semaphore_signal(barrier, inc=1, device_id=kind(i), device_id_type=MESH)
            return c
        lax.fori_loop(1, count, body, 0)

    def z_peer(i):
        return {"ctx": y * NZ + lax.rem(z + i, NZ)}

    def y_peer(i):
        return {"ctx": lax.rem(y + i, NY) * NZ + z}

    def h_peer(i):
        return {"head": lax.rem(me + i, NH)}

    greet(z_peer, NZ)
    greet(y_peer, NY)
    greet(h_peer, NH)

    lane = lax.broadcasted_iota(jnp.int32, (tok, LANES), 1)
    low = lane < DH

    def prepare(both, x_ref, z_ref):
        swapped = pltpu.roll(both, DH, 1)
        for h in range(2):
            xx = jnp.where(low, both, swapped) if h == 0 else jnp.where(low, swapped, both)
            x_ref[h] = xx
            z_ref[h] = jnp.where(low, xx, pltpu.roll(xx, DH // 2, 1))

    def product(x_ref, z_ref, h, distance):
        return (z_ref[h] * pltpu.roll(x_ref[h], lax.rem(LANES - distance, LANES), 1)).astype(BF16)

    def middle(both, x_ref):
        shifted = jnp.where(low, pltpu.roll(x_ref[0], LANES - 16, 1), pltpu.roll(x_ref[1], LANES - 16, 1))
        return both * shifted

    keys32 = k_ref[...].astype(F32)
    prepare(keys32, kx, kz)
    vt[...] = jnp.transpose(v_ref[...].astype(F32)).astype(BF16)

    def states(r):
        h, half = r // 2, r % 2
        def body(i, c):
            first = half * 8 + 2 * i
            feats = jnp.concatenate(
                [product(kx, kz, h, first), product(kx, kz, h, first + 1)], axis=1)
            state = nn(vt[h * DH:(h + 1) * DH, :], feats).astype(BF16)
            send1[r, 2 * i, 0:DH, :] = state[:, :LANES]
            send1[r, 2 * i + 1, 0:DH, :] = state[:, LANES:]
            return c
        lax.fori_loop(0, NZ // 2, body, 0)

    def extra_state():
        feats = middle(k_ref[...].astype(F32), kx).astype(BF16)
        pair = nn(vt[...], feats)
        state = jnp.where(low[:DH], pair[:DH], pair[DH:])
        for o in range(NZ):
            piece = jnp.concatenate([state[8 * o:8 * o + 8], jnp.zeros((8, LANES), F32)], axis=0)
            send1[0, o, DH:DH + EXTRA, :] = piece.astype(BF16)

    def columns(i):
        return pl.ds(pl.multiple_of(i * LANES, LANES), LANES)

    def copy(src, dst, sends, recvs, peer):
        return pltpu.make_async_remote_copy(
            src_ref=src, dst_ref=dst, send_sem=sends, recv_sem=recvs, device_id=peer, device_id_type=MESH)

    def z_from(i, arriving):
        return lax.rem(z + NZ - i, NZ) if arriving else z

    def copy1(r, i, arriving=False):
        o, s, n = lax.rem(z + i, NZ), z_from(i, arriving), rows_of(r)
        return copy(send1.at[r, o, pl.ds(0, n)], recv1.at[r, s, pl.ds(0, n)],
                    s1_send.at[r, o], s1_recv.at[r, s], z_peer(i))

    def copy2(r, i, arriving=False):
        o, s, n = lax.rem(z + i, NZ), z_from(i, arriving), rows_of(r)
        return copy(send2.at[r, o, pl.ds(0, n)], recv2.at[r, s, pl.ds(0, n)],
                    s2_send.at[r, o], s2_recv.at[r, s], z_peer(i))

    def copy_y(r, i, arriving=False):
        o, n = lax.rem(y + i, NY), rows_of(r)
        s = lax.rem(y + NY - i, NY) if arriving else y
        return copy(ybuf.at[r, y, pl.ds(0, n)], ybuf.at[r, s, pl.ds(0, n)],
                    y_send.at[r, o], y_recv.at[r, s], y_peer(i))

    def head_from(i, arriving):
        return lax.rem(me + NH - i, NH) if arriving else me

    def copy_w(i, arriving=False):
        o, s = lax.rem(me + i, NH), head_from(i, arriving)
        return copy(w_ref.at[:, columns(o)], wbuf.at[s], w_send.at[o], w_recv.at[s], h_peer(i))

    def copy_n(h, i, arriving=False):
        o, s = lax.rem(me + i, NH), head_from(i, arriving)
        return copy(ncat.at[h, me], ncat.at[h, s], n_send.at[h, o], n_recv.at[h, s], h_peer(i))

    def each(count, do):
        def body(i, c):
            do(i)
            return c
        lax.fori_loop(1, count, body, 0)

    extra_state()
    for r in range(ROUNDS):
        states(r)
        if r == 0:
            pl.semaphore_wait(barrier, NZ + NY + NH - 3)
        each(NZ, lambda i: copy1(r, i).start())
        recv1[r, z, 0:rows_of(r), :] = send1[r, z, 0:rows_of(r), :]
    each(NH, lambda i: copy_w(i).start())
    wbuf[me] = w_ref[:, columns(me)]

    queries32 = q_ref[...].astype(F32) * 0.125
    prepare(queries32, qx, qz)
    for h in range(2):
        qf[h, 0] = product(qx, qz, h, 0)
        qz[h] = qz[h] * 2.0
        mine = low if h == 0 else jnp.logical_not(low)
        qf[h, 16] = jnp.where(mine, middle(queries32 * 2.0, qx), 0.0).astype(BF16)

        def fill(i, c, h=h):
            qf[h, i] = product(qx, qz, h, i)
            return c
        lax.fori_loop(1, 16, fill, 0)

    def intra(h):
        mine = low if h == 0 else jnp.logical_not(low)
        masked = jnp.where(mine, queries32, 0.0).astype(BF16)
        for b in range(2):
            seen, first = 256 * (b + 1), 256 * b
            scores = nt(k_ref[0:seen, :], masked[first:first + 256])
            s_at = lax.broadcasted_iota(jnp.int32, (seen, 256), 0)
            t_at = lax.broadcasted_iota(jnp.int32, (seen, 256), 1) + first
            weights = jnp.where(s_at <= t_at, scores * scores, 0.0).astype(BF16)
            num[h, :, first:first + 256] = nn(vt[h * DH:(h + 1) * DH, 0:seen], weights)

    intra(0)
    intra(1)

    def totals(r):
        n = rows_of(r)
        each(NZ, lambda i: copy1(r, i, True).wait_recv())
        total = recv1[r, 0, 0:n, :].astype(F32)
        for s in range(1, NZ):
            total += recv1[r, s, 0:n, :].astype(F32)
        ybuf[r, y, 0:n, :] = total
        each(NY, lambda i: copy_y(r, i).start())

    def prefixes(r):
        n = rows_of(r)
        each(NY, lambda i: copy_y(r, i, True).wait_recv())
        running = jnp.zeros((n, LANES), F32)
        for s in range(NY):
            running += jnp.where(s < y, ybuf[r, s, 0:n, :], 0.0)
        for s in range(NZ):
            send2[r, s, 0:n, :] = running.astype(BF16)
            running += recv1[r, s, 0:n, :].astype(F32)
        each(NZ, lambda i: copy2(r, i).start())
        recv2[r, z, 0:n, :] = send2[r, z, 0:n, :]

    def read_out(r):
        h, half = r // 2, r % 2
        each(NZ, lambda i: copy2(r, i, True).wait_recv())
        prefix = [recv2[r, o, 0:DH, :] for o in range(NZ)]
        feats = [qf[h, half * 8 + o] for o in range(NZ)]
        if half == 0:
            pieces = [recv2[0, o, DH:DH + EXTRA, :].astype(F32)[:8] for o in range(NZ)]
            prefix.append(jnp.concatenate(pieces, axis=0).astype(BF16))
            feats.append(qf[h, 16])
        num[h] += nt(jnp.concatenate(prefix, axis=1), jnp.concatenate(feats, axis=1))

    gains = jnp.transpose(jnp.broadcast_to(gain_ref[...], (LANES, LANES)))

    def normalise(h):
        value = num[h]
        meansq = jnp.mean(value * value, axis=0, keepdims=True)
        gain = jnp.concatenate([gains[h * DH:(h + 1) * DH]] * (tok // LANES), axis=1)
        ncat[h, me] = (value * lax.rsqrt(meansq + EPSILON) * gain).astype(BF16)
        each(NH, lambda i: copy_n(h, i).start())

    totals(0)
    totals(1)
    prefixes(0)
    totals(2)
    prefixes(1)
    totals(3)
    prefixes(2)
    each(NH, lambda i: copy_w(i, True).wait_recv())
    for s in range(NH):
        wt[:, s * LANES:(s + 1) * LANES] = jnp.transpose(wbuf[s].astype(F32)).astype(BF16)
    prefixes(3)
    read_out(0)
    read_out(1)
    normalise(0)
    read_out(2)
    read_out(3)
    normalise(1)
    for h in range(2):
        each(NH, lambda i: copy_n(h, i, True).wait_recv())
    blocks = jnp.concatenate([ncat[h, s] for s in range(NH) for h in range(2)], axis=0)
    mixed = nn(wt[...], blocks)
    out_ref[...] = jnp.transpose(mixed).astype(BF16)

    for r in range(ROUNDS):
        each(NZ, lambda i: copy1(r, i).wait_send())
        each(NY, lambda i: copy_y(r, i).wait_send())
        each(NZ, lambda i: copy2(r, i).wait_send())
    each(NH, lambda i: copy_w(i).wait_send())
    for h in range(2):
        each(NH, lambda i: copy_n(h, i).wait_send())


def per_device(queries, keys, values, gain, out_weight):
    tok, width = queries.shape
    rows = DH + EXTRA
    vmem = pl.BlockSpec(memory_space=pltpu.VMEM)
    dma = pltpu.SemaphoreType.DMA
    return pl.pallas_call(
        kernel,
        out_shape=jax.ShapeDtypeStruct((tok, width), BF16),
        in_specs=[vmem] * 5,
        out_specs=vmem,
        scratch_shapes=[
            pltpu.VMEM((2, tok, LANES), F32),
            pltpu.VMEM((2, tok, LANES), F32),
            pltpu.VMEM((2, tok, LANES), F32),
            pltpu.VMEM((2, tok, LANES), F32),
            pltpu.VMEM((LANES, tok), BF16),
            pltpu.VMEM((2, 17, tok, LANES), BF16),
            pltpu.VMEM((2, DH, tok), F32),
            pltpu.VMEM((NH, LANES, LANES), BF16),
            pltpu.VMEM((LANES, NH * LANES), BF16),
            pltpu.VMEM((2, NH, DH, tok), BF16),
            pltpu.VMEM((ROUNDS, NZ, rows, LANES), BF16),
            pltpu.VMEM((ROUNDS, NZ, rows, LANES), BF16),
            pltpu.VMEM((ROUNDS, NY, rows, LANES), F32),
            pltpu.VMEM((ROUNDS, NZ, rows, LANES), BF16),
            pltpu.VMEM((ROUNDS, NZ, rows, LANES), BF16),
            dma((ROUNDS, NZ)), dma((ROUNDS, NZ)),
            dma((ROUNDS, NY)), dma((ROUNDS, NY)),
            dma((ROUNDS, NZ)), dma((ROUNDS, NZ)),
            dma((NH,)), dma((NH,)),
            dma((2, NH)), dma((2, NH)),
        ],
        compiler_params=pltpu.CompilerParams(
            collective_id=0, has_side_effects=True, vmem_limit_bytes=40 << 20),
    )(queries, keys, values, gain.reshape(1, width), out_weight)


def solution(mesh):
    return jax.shard_map(
        per_device,
        mesh=mesh,
        in_specs=(P("ctx", "head"), P("ctx", "head"), P("ctx", "head"), P("head"), P("head", None)),
        out_specs=P("ctx", "head"),
        check_vma=False,
    )
```

```python
import functools

import jax
import jax.numpy as jnp
from jax import lax
from jax.experimental import pallas as pl
from jax.experimental.pallas import tpu as pltpu
from jax.sharding import PartitionSpec as P

MESH = pl.DeviceIdType.MESH
DH = 64
LANES = 128
EPSILON = 1e-06
NZ = 8
NY = 4
NH = 8
ROUNDS = 4
EXTRA = 16
F32 = jnp.float32
BF16 = jnp.bfloat16


def nt(a, b):
    return lax.dot_general(a, b, (((1,), (1,)), ((), ())), preferred_element_type=F32)


def nn(a, b):
    return lax.dot_general(a, b, (((1,), (0,)), ((), ())), preferred_element_type=F32)


def rows_of(r):
    return DH + EXTRA if r == 0 else DH


def kernel(q_hbm, k_hbm, v_hbm, gain_hbm, w_hbm, out_ref,
           q_ref, k_ref, v_ref, gain_ref, w_ref, kx, kz, qx, qz, vt, qf, num, wbuf, wt, acc, ncat, send1, recv1, ybuf, send2, recv2,
           s1_send, s1_recv, y_send, y_recv, s2_send, s2_recv, w_send, w_recv, n_send, n_recv, p_send, loaded):
    ctx = lax.axis_index("ctx")
    y, z = ctx // NZ, lax.rem(ctx, NZ)
    me = lax.axis_index("head")
    tok = q_ref.shape[0]

    def load(i):
        pairs = ((k_hbm, k_ref), (v_hbm, v_ref), (q_hbm, q_ref), (w_hbm, w_ref), (gain_hbm, gain_ref))
        return pltpu.make_async_copy(*pairs[i], loaded.at[i])

    for i in range(5):
        load(i).start()

    barrier = pltpu.get_barrier_semaphore()

    def greet(kind, count):
        def body(i, c):
            pl.semaphore_signal(barrier, inc=1, device_id=kind(i), device_id_type=MESH)
            return c
        lax.fori_loop(1, count, body, 0)

    def z_peer(i):
        return {"ctx": y * NZ + lax.rem(z + i, NZ)}

    def y_peer(i):
        return {"ctx": lax.rem(y + i, NY) * NZ + z}

    def h_peer(i):
        return {"head": lax.rem(me + i, NH)}

    greet(z_peer, NZ)
    greet(y_peer, NY)
    greet(h_peer, NH)

    lane = lax.broadcasted_iota(jnp.int32, (tok, LANES), 1)
    low = lane < DH

    def prepare(both, x_ref, z_ref):
        swapped = pltpu.roll(both, DH, 1)
        for h in range(2):
            xx = jnp.where(low, both, swapped) if h == 0 else jnp.where(low, swapped, both)
            x_ref[h] = xx
            z_ref[h] = jnp.where(low, xx, pltpu.roll(xx, DH // 2, 1))

    def products(x_ref, z_ref, h, first, count):
        fixed = z_ref[h].astype(BF16)
        turned = [pltpu.roll(x_ref[h], (LANES - d) % LANES, 1) for d in range(first, first + count)]
        return [fixed * t.astype(BF16) for t in turned]

    def middle(both, x_ref):
        shifted = jnp.where(low, pltpu.roll(x_ref[0], LANES - 16, 1), pltpu.roll(x_ref[1], LANES - 16, 1))
        return both * shifted

    load(0).wait()
    keys32 = k_ref[...].astype(F32)
    prepare(keys32, kx, kz)
    load(1).wait()
    vt[...] = jnp.transpose(v_ref[...].astype(F32)).astype(BF16)

    def states(r):
        h, half = r // 2, r % 2
        feats = jnp.concatenate(products(kx, kz, h, half * NZ, NZ), axis=1)
        state = nn(vt[h * DH:(h + 1) * DH, :], feats).astype(BF16)
        for o in range(NZ):
            send1[r, o, 0:DH, :] = state[:, o * LANES:(o + 1) * LANES]

    def extra_state():
        feats = middle(k_ref[...].astype(F32), kx).astype(BF16)
        pair = nn(vt[...], feats)
        state = jnp.where(low[:DH], pair[:DH], pair[DH:])
        for o in range(NZ):
            piece = jnp.concatenate([state[8 * o:8 * o + 8], jnp.zeros((8, LANES), F32)], axis=0)
            send1[0, o, DH:DH + EXTRA, :] = piece.astype(BF16)

    def columns(i):
        return pl.ds(pl.multiple_of(i * LANES, LANES), LANES)

    def copy(src, dst, sends, recvs, peer):
        return pltpu.make_async_remote_copy(
            src_ref=src, dst_ref=dst, send_sem=sends, recv_sem=recvs, device_id=peer, device_id_type=MESH)

    def z_from(i, arriving):
        return lax.rem(z + NZ - i, NZ) if arriving else z

    def copy1(r, i, arriving=False):
        o, s, n = lax.rem(z + i, NZ), z_from(i, arriving), rows_of(r)
        return copy(send1.at[r, o, pl.ds(0, n)], recv1.at[r, s, pl.ds(0, n)],
                    s1_send.at[r, o], s1_recv.at[r, s], z_peer(i))

    def copy2(r, i, arriving=False):
        o, s, n = lax.rem(z + i, NZ), z_from(i, arriving), rows_of(r)
        return copy(send2.at[r, o, pl.ds(0, n)], recv2.at[r, s, pl.ds(0, n)],
                    s2_send.at[r, o], s2_recv.at[r, s], z_peer(i))

    def copy_y(r, i, arriving=False):
        o, n = lax.rem(y + i, NY), rows_of(r)
        s = lax.rem(y + NY - i, NY) if arriving else y
        return copy(ybuf.at[r, y, pl.ds(0, n)], ybuf.at[r, s, pl.ds(0, n)],
                    y_send.at[r, o], y_recv.at[r, s], y_peer(i))

    def head_from(i, arriving):
        return lax.rem(me + NH - i, NH) if arriving else me

    def copy_w(i, arriving=False):
        o, s = lax.rem(me + i, NH), head_from(i, arriving)
        return copy(w_ref.at[:, columns(o)], wbuf.at[s], w_send.at[o], w_recv.at[s], h_peer(i))

    def copy_n(h, i, arriving=False):
        s = head_from(2 * i, arriving)
        return copy(ncat.at[h, me], ncat.at[h, s], n_send.at[h, i], n_recv.at[h, s], h_peer(2 * i))

    sibling = {"head": me + 1 - 2 * lax.rem(me, 2)}

    def copy_pair(h, i, arriving=False):
        held = lax.rem(me + NH - 2 * i, NH)
        s = held + 1 - 2 * lax.rem(me, 2) if arriving else held
        return copy(ncat.at[h, held], ncat.at[h, s], p_send.at[h, i], n_recv.at[h, s], sibling)

    def each(count, do):
        def body(i, c):
            do(i)
            return c
        lax.fori_loop(1, count, body, 0)

    extra_state()
    for r in range(ROUNDS):
        states(r)
        if r == 0:
            pl.semaphore_wait(barrier, NZ + NY + NH - 3)
        each(NZ, lambda i: copy1(r, i).start())
        recv1[r, z, 0:rows_of(r), :] = send1[r, z, 0:rows_of(r), :]
    load(3).wait()
    each(NH, lambda i: copy_w(i).start())
    wbuf[me] = w_ref[:, columns(me)]

    load(2).wait()
    queries32 = q_ref[...].astype(F32) * 0.125
    prepare(queries32, qx, qz)
    for h in range(2):
        mine = low if h == 0 else jnp.logical_not(low)
        qf[h, 16] = jnp.where(mine, middle(queries32 * 2.0, qx), 0.0).astype(BF16)
        qf[h, 0] = products(qx, qz, h, 0, 1)[0]
        qz[h] = qz[h] * 2.0
        for i, feats in enumerate(products(qx, qz, h, 1, 15)):
            qf[h, i + 1] = feats

    def intra(h):
        mine = low if h == 0 else jnp.logical_not(low)
        masked = jnp.where(mine, queries32, 0.0).astype(BF16)
        for b in range(2):
            seen, first = 256 * (b + 1), 256 * b
            scores = nt(k_ref[0:seen, :], masked[first:first + 256])
            s_at = lax.broadcasted_iota(jnp.int32, (seen, 256), 0)
            t_at = lax.broadcasted_iota(jnp.int32, (seen, 256), 1) + first
            weights = jnp.where(s_at <= t_at, scores * scores, 0.0).astype(BF16)
            num[h, :, first:first + 256] = nn(vt[h * DH:(h + 1) * DH, 0:seen], weights)

    intra(0)
    intra(1)

    def totals(r):
        n = rows_of(r)
        each(NZ, lambda i: copy1(r, i, True).wait_recv())
        total = recv1[r, 0, 0:n, :].astype(F32)
        for s in range(1, NZ):
            total += recv1[r, s, 0:n, :].astype(F32)
        ybuf[r, y, 0:n, :] = total
        def to_later(i):
            @pl.when(y + i < NY)
            def _():
                copy_y(r, i).start()
        each(NY, to_later)

    def prefixes(r):
        n = rows_of(r)
        def from_earlier(i):
            @pl.when(y >= i)
            def _():
                copy_y(r, i, True).wait_recv()
        each(NY, from_earlier)
        running = jnp.zeros((n, LANES), F32)
        for s in range(NY):
            running += jnp.where(s < y, ybuf[r, s, 0:n, :], 0.0)
        for s in range(NZ):
            send2[r, s, 0:n, :] = running.astype(BF16)
            running += recv1[r, s, 0:n, :].astype(F32)
        def give(i):
            @pl.when(y + lax.rem(z + i, NZ) > 0)
            def _():
                copy2(r, i).start()
        each(NZ, give)
        recv2[r, z, 0:n, :] = send2[r, z, 0:n, :]

    def read_out(r):
        h, half = r // 2, r % 2
        @pl.when(y + z > 0)
        def _():
            each(NZ, lambda i: copy2(r, i, True).wait_recv())

        @pl.when(y + z == 0)
        def _():
            recv2[r] = jnp.zeros(recv2.shape[1:], BF16)
        prefix = [recv2[r, o, 0:DH, :] for o in range(NZ)]
        feats = [qf[h, half * 8 + o] for o in range(NZ)]
        if half == 0:
            pieces = [recv2[0, o, DH:DH + EXTRA, :].astype(F32)[:8] for o in range(NZ)]
            prefix.append(jnp.concatenate(pieces, axis=0).astype(BF16))
            feats.append(qf[h, 16])
        num[h] += nt(jnp.concatenate(prefix, axis=1), jnp.concatenate(feats, axis=1))

    load(4).wait()
    gains = jnp.transpose(jnp.broadcast_to(gain_ref[...], (LANES, LANES)))

    def normalise(h):
        value = num[h]
        meansq = jnp.mean(value * value, axis=0, keepdims=True)
        gain = jnp.concatenate([gains[h * DH:(h + 1) * DH]] * (tok // LANES), axis=1)
        ncat[h, me] = (value * lax.rsqrt(meansq + EPSILON) * gain).astype(BF16)
        each(NH // 2, lambda i: copy_n(h, i).start())
        copy_pair(h, 0).start()

    def pass_on(h):
        for i in (1, 3, 2):
            copy_n(h, i, True).wait_recv()
            copy_pair(h, i).start()

    def project(h):
        for i in range(NH // 2):
            copy_pair(h, i, True).wait_recv()
        blocks = jnp.concatenate([ncat[h, s] for s in range(NH)], axis=0)
        return nn(wt[:, h * NH * DH:(h + 1) * NH * DH], blocks)

    totals(0)
    totals(1)
    prefixes(0)
    totals(2)
    prefixes(1)
    totals(3)
    prefixes(2)
    each(NH, lambda i: copy_w(i, True).wait_recv())
    turned = [jnp.transpose(wbuf[s].astype(F32)) for s in range(NH)]
    for h in range(2):
        part = jnp.concatenate([t[:, h * DH:(h + 1) * DH] for t in turned], axis=1)
        wt[:, h * NH * DH:(h + 1) * NH * DH] = part.astype(BF16)
    prefixes(3)
    read_out(0)
    read_out(1)
    normalise(0)
    read_out(2)
    pass_on(0)
    read_out(3)
    normalise(1)
    acc[...] = project(0)
    pass_on(1)
    out_ref[...] = jnp.transpose(acc[...] + project(1)).astype(BF16)

    for r in range(ROUNDS):
        each(NZ, lambda i: copy1(r, i).wait_send())
        def sent(i, r=r):
            @pl.when(y + i < NY)
            def _():
                copy_y(r, i).wait_send()
        each(NY, sent)
        def given(i, r=r):
            @pl.when(y + lax.rem(z + i, NZ) > 0)
            def _():
                copy2(r, i).wait_send()
        each(NZ, given)
    each(NH, lambda i: copy_w(i).wait_send())
    for h in range(2):
        each(NH // 2, lambda i: copy_n(h, i).wait_send())
        for i in range(NH // 2):
            copy_pair(h, i).wait_send()


def per_device(queries, keys, values, gain, out_weight):
    tok, width = queries.shape
    rows = DH + EXTRA
    vmem = pl.BlockSpec(memory_space=pltpu.VMEM)
    dma = pltpu.SemaphoreType.DMA
    return pl.pallas_call(
        kernel,
        out_shape=jax.ShapeDtypeStruct((tok, width), BF16),
        in_specs=[pl.BlockSpec(memory_space=pltpu.HBM)] * 5,
        out_specs=vmem,
        scratch_shapes=[
            pltpu.VMEM((tok, width), BF16),
            pltpu.VMEM((tok, width), BF16),
            pltpu.VMEM((tok, width), BF16),
            pltpu.VMEM((1, width), F32),
            pltpu.VMEM(out_weight.shape, BF16),
            pltpu.VMEM((2, tok, LANES), F32),
            pltpu.VMEM((2, tok, LANES), F32),
            pltpu.VMEM((2, tok, LANES), F32),
            pltpu.VMEM((2, tok, LANES), F32),
            pltpu.VMEM((LANES, tok), BF16),
            pltpu.VMEM((2, 17, tok, LANES), BF16),
            pltpu.VMEM((2, DH, tok), F32),
            pltpu.VMEM((NH, LANES, LANES), BF16),
            pltpu.VMEM((LANES, NH * LANES), BF16),
            pltpu.VMEM((LANES, tok), F32),
            pltpu.VMEM((2, NH, DH, tok), BF16),
            pltpu.VMEM((ROUNDS, NZ, rows, LANES), BF16),
            pltpu.VMEM((ROUNDS, NZ, rows, LANES), BF16),
            pltpu.VMEM((ROUNDS, NY, rows, LANES), F32),
            pltpu.VMEM((ROUNDS, NZ, rows, LANES), BF16),
            pltpu.VMEM((ROUNDS, NZ, rows, LANES), BF16),
            dma((ROUNDS, NZ)), dma((ROUNDS, NZ)),
            dma((ROUNDS, NY)), dma((ROUNDS, NY)),
            dma((ROUNDS, NZ)), dma((ROUNDS, NZ)),
            dma((NH,)), dma((NH,)),
            dma((2, NH // 2)), dma((2, NH)), dma((2, NH // 2)),
            dma((5,)),
        ],
        compiler_params=pltpu.CompilerParams(
            collective_id=0, has_side_effects=True, vmem_limit_bytes=55040 << 10),
    )(queries, keys, values, gain.reshape(1, width), out_weight)


def solution(mesh):
    return jax.shard_map(
        per_device,
        mesh=mesh,
        in_specs=(P("ctx", "head"), P("ctx", "head"), P("ctx", "head"), P("head"), P("head", None)),
        out_specs=P("ctx", "head"),
        check_vma=False,
    )
```

```python
import functools

import jax
import jax.numpy as jnp
from jax import lax
from jax.experimental import pallas as pl
from jax.experimental.pallas import tpu as pltpu
from jax.sharding import PartitionSpec as P

MESH = pl.DeviceIdType.MESH
DH = 64
LANES = 128
EPSILON = 1e-06
NZ = 8
NY = 4
NH = 8
ROUNDS = 4
EXTRA = 16
F32 = jnp.float32
BF16 = jnp.bfloat16


def nt(a, b):
    return lax.dot_general(a, b, (((1,), (1,)), ((), ())), preferred_element_type=F32)


def nn(a, b):
    return lax.dot_general(a, b, (((1,), (0,)), ((), ())), preferred_element_type=F32)


FIRST = 48
ROWS = (DH + EXTRA, DH, 2 * FIRST, 2 * (DH - FIRST))


def rows_of(r):
    return ROWS[r]


def kernel(q_hbm, k_hbm, v_hbm, gain_hbm, w_hbm, out_ref,
           q_ref, k_ref, v_ref, gain_ref, w_ref, kx, kz, qx, qz, vt, qf, num, wbuf, wt, wt2, acc, middles, ncat, early, last, send1, recv1, ybuf, send2, recv2,
           s1_send, s1_recv, y_send, y_recv, s2_send, s2_recv, w_send, w_recv, n_send, n_recv, p_send, l_send, l_recv, loaded):
    ctx = lax.axis_index("ctx")
    y, z = ctx // NZ, lax.rem(ctx, NZ)
    me = lax.axis_index("head")
    tok = q_ref.shape[0]

    def load(i):
        pairs = ((k_hbm, k_ref), (v_hbm, v_ref), (q_hbm, q_ref), (w_hbm, w_ref), (gain_hbm, gain_ref))
        return pltpu.make_async_copy(*pairs[i], loaded.at[i])

    for i in range(5):
        load(i).start()

    barrier = pltpu.get_barrier_semaphore()

    def greet(kind, count):
        def body(i, c):
            pl.semaphore_signal(barrier, inc=1, device_id=kind(i), device_id_type=MESH)
            return c
        lax.fori_loop(1, count, body, 0)

    def z_peer(i):
        return {"ctx": y * NZ + lax.rem(z + i, NZ)}

    def y_peer(i):
        return {"ctx": lax.rem(y + i, NY) * NZ + z}

    def h_peer(i):
        return {"head": lax.rem(me + i, NH)}

    greet(z_peer, NZ)
    greet(y_peer, NY)
    greet(h_peer, NH)

    lane = lax.broadcasted_iota(jnp.int32, (tok, LANES), 1)
    low = lane < DH

    def prepare(both, x_ref, z_ref):
        swapped = pltpu.roll(both, DH, 1)
        for h in range(2):
            xx = jnp.where(low, both, swapped) if h == 0 else jnp.where(low, swapped, both)
            x_ref[h] = xx
            z_ref[h] = jnp.where(low, xx, pltpu.roll(xx, DH // 2, 1))

    def products(x_ref, z_ref, h, first, count):
        fixed = z_ref[h].astype(BF16)
        turned = [pltpu.roll(x_ref[h], (LANES - d) % LANES, 1) for d in range(first, first + count)]
        return [fixed * t.astype(BF16) for t in turned]

    def middle(both, x_ref):
        shifted = jnp.where(low, pltpu.roll(x_ref[0], LANES - 16, 1), pltpu.roll(x_ref[1], LANES - 16, 1))
        return both * shifted

    load(0).wait()
    keys32 = k_ref[...].astype(F32)
    prepare(keys32, kx, kz)
    load(1).wait()
    vt[...] = jnp.transpose(v_ref[...].astype(F32)).astype(BF16)

    def states(h, half):
        feats = jnp.concatenate(products(kx, kz, h, half * NZ, NZ), axis=1)
        state = nn(vt[h * DH:(h + 1) * DH, :], feats).astype(BF16)
        for o in range(NZ):
            piece = state[:, o * LANES:(o + 1) * LANES]
            if h == 0:
                send1[half, o, 0:DH, :] = piece
            else:
                last = DH - FIRST
                send1[2, o, half * FIRST:(half + 1) * FIRST, :] = piece[:FIRST]
                send1[3, o, half * last:(half + 1) * last, :] = piece[FIRST:]

    def extra_state():
        feats = middle(k_ref[...].astype(F32), kx).astype(BF16)
        pair = nn(vt[...], feats)
        state = jnp.where(low[:DH], pair[:DH], pair[DH:])
        for o in range(NZ):
            piece = jnp.concatenate([state[8 * o:8 * o + 8], jnp.zeros((8, LANES), F32)], axis=0)
            send1[0, o, DH:DH + EXTRA, :] = piece.astype(BF16)

    def columns(i):
        return pl.ds(pl.multiple_of(i * LANES, LANES), LANES)

    def copy(src, dst, sends, recvs, peer):
        return pltpu.make_async_remote_copy(
            src_ref=src, dst_ref=dst, send_sem=sends, recv_sem=recvs, device_id=peer, device_id_type=MESH)

    def z_from(i, arriving):
        return lax.rem(z + NZ - i, NZ) if arriving else z

    def copy1(r, i, arriving=False):
        o, s, n = lax.rem(z + i, NZ), z_from(i, arriving), rows_of(r)
        return copy(send1.at[r, o, pl.ds(0, n)], recv1.at[r, s, pl.ds(0, n)],
                    s1_send.at[r, o], s1_recv.at[r, s], z_peer(i))

    def copy2(r, i, arriving=False):
        o, s, n = lax.rem(z + i, NZ), z_from(i, arriving), rows_of(r)
        return copy(send2.at[r, o, pl.ds(0, n)], recv2.at[r, s, pl.ds(0, n)],
                    s2_send.at[r, o], s2_recv.at[r, s], z_peer(i))

    def copy_y(r, i, arriving=False):
        o, n = lax.rem(y + i, NY), rows_of(r)
        s = lax.rem(y + NY - i, NY) if arriving else y
        return copy(ybuf.at[r, y, pl.ds(0, n)], ybuf.at[r, s, pl.ds(0, n)],
                    y_send.at[r, o], y_recv.at[r, s], y_peer(i))

    def head_from(i, arriving):
        return lax.rem(me + NH - i, NH) if arriving else me

    def copy_w(i, arriving=False):
        o, s = lax.rem(me + i, NH), head_from(i, arriving)
        return copy(w_ref.at[:, columns(o)], wbuf.at[s], w_send.at[o], w_recv.at[s], h_peer(i))

    def copy_n(h, i, arriving=False):
        s, held = head_from(2 * i, arriving), (ncat, early)[h]
        return copy(held.at[me], held.at[s], n_send.at[h, i], n_recv.at[h, s], h_peer(2 * i))

    sibling = {"head": me + 1 - 2 * lax.rem(me, 2)}

    def copy_pair(h, i, arriving=False):
        mine, held = lax.rem(me + NH - 2 * i, NH), (ncat, early)[h]
        s = mine + 1 - 2 * lax.rem(me, 2) if arriving else mine
        return copy(held.at[mine], held.at[s], p_send.at[h, i], n_recv.at[h, s], sibling)

    def copy_last(i, arriving=False):
        s = head_from(i, arriving)
        return copy(last.at[me], last.at[s], l_send.at[i], l_recv.at[s], h_peer(i))

    def each(count, do):
        def body(i, c):
            do(i)
            return c
        lax.fori_loop(1, count, body, 0)

    extra_state()
    for r in range(ROUNDS):
        if r < 2:
            states(0, r)
        elif r == 2:
            states(1, 0)
            states(1, 1)
        if r == 0:
            pl.semaphore_wait(barrier, NZ + NY + NH - 3)
        each(NZ, lambda i: copy1(r, i).start())
        recv1[r, z, 0:rows_of(r), :] = send1[r, z, 0:rows_of(r), :]
    load(3).wait()
    each(NH, lambda i: copy_w(i).start())
    wbuf[me] = w_ref[:, columns(me)]

    load(2).wait()
    queries32 = q_ref[...].astype(F32) * 0.125
    prepare(queries32, qx, qz)
    for h in range(2):
        mine = low if h == 0 else jnp.logical_not(low)
        qf[h, 16] = jnp.where(mine, middle(queries32 * 2.0, qx), 0.0).astype(BF16)
        qf[h, 0] = products(qx, qz, h, 0, 1)[0]
        qz[h] = qz[h] * 2.0
        for i, feats in enumerate(products(qx, qz, h, 1, 15)):
            qf[h, i + 1] = feats

    def intra(h):
        mine = low if h == 0 else jnp.logical_not(low)
        masked = jnp.where(mine, queries32, 0.0).astype(BF16)
        for b in range(2):
            seen, first = 256 * (b + 1), 256 * b
            scores = nt(k_ref[0:seen, :], masked[first:first + 256])
            s_at = lax.broadcasted_iota(jnp.int32, (seen, 256), 0)
            t_at = lax.broadcasted_iota(jnp.int32, (seen, 256), 1) + first
            weights = jnp.where(s_at <= t_at, scores * scores, 0.0).astype(BF16)
            num[h, :, first:first + 256] = nn(vt[h * DH:(h + 1) * DH, 0:seen], weights)

    intra(0)
    intra(1)

    def totals(r):
        n = rows_of(r)
        each(NZ, lambda i: copy1(r, i, True).wait_recv())
        total = recv1[r, 0, 0:n, :].astype(F32)
        for s in range(1, NZ):
            total += recv1[r, s, 0:n, :].astype(F32)
        ybuf[r, y, 0:n, :] = total
        def to_later(i):
            @pl.when(y + i < NY)
            def _():
                copy_y(r, i).start()
        each(NY, to_later)

    def prefixes(r):
        n = rows_of(r)
        def from_earlier(i):
            @pl.when(y >= i)
            def _():
                copy_y(r, i, True).wait_recv()
        each(NY, from_earlier)
        running = jnp.zeros((n, LANES), F32)
        for s in range(NY):
            running += jnp.where(s < y, ybuf[r, s, 0:n, :], 0.0)
        for s in range(NZ):
            send2[r, s, 0:n, :] = running.astype(BF16)
            running += recv1[r, s, 0:n, :].astype(F32)
        def give(i):
            @pl.when(y + lax.rem(z + i, NZ) > 0)
            def _():
                copy2(r, i).start()
        each(NZ, give)
        recv2[r, z, 0:n, :] = send2[r, z, 0:n, :]

    def arrived(r):
        @pl.when(y + z > 0)
        def _():
            each(NZ, lambda i: copy2(r, i, True).wait_recv())

        @pl.when(y + z == 0)
        def _():
            recv2[r] = jnp.zeros(recv2.shape[1:], BF16)

    def read_out_first(half):
        arrived(half)
        prefix = [recv2[half, o, 0:DH, :] for o in range(NZ)]
        feats = [qf[0, half * NZ + o] for o in range(NZ)]
        if half == 0:
            pieces = [recv2[0, o, DH:DH + EXTRA, :].astype(F32)[:8] for o in range(NZ)]
            middles[...] = jnp.concatenate(pieces, axis=0).astype(BF16)
            prefix.append(middles[...])
            feats.append(qf[0, 16])
        num[0] += nt(jnp.concatenate(prefix, axis=1), jnp.concatenate(feats, axis=1))

    def read_out_second(r):
        first, n = (0, FIRST) if r == 2 else (FIRST, DH - FIRST)
        arrived(r)
        prefix = [recv2[r, o, half * n:(half + 1) * n, :] for half in range(2) for o in range(NZ)]
        prefix.append(middles[first:first + n, :])
        feats = [qf[1, i] for i in range(17)]
        num[1, first:first + n, :] += nt(jnp.concatenate(prefix, axis=1), jnp.concatenate(feats, axis=1))

    load(4).wait()
    gains = jnp.transpose(jnp.broadcast_to(gain_ref[...], (LANES, LANES)))

    def gain_of(first, n):
        return jnp.concatenate([gains[first:first + n]] * (tok // LANES), axis=1)

    def inverse_norm(h):
        value = num[h]
        return lax.rsqrt(jnp.mean(value * value, axis=0, keepdims=True) + EPSILON)

    def spread(h):
        each(NH // 2, lambda i: copy_n(h, i).start())
        copy_pair(h, 0).start()

    def give_first():
        ncat[me] = (num[0] * inverse_norm(0) * gain_of(0, DH)).astype(BF16)
        spread(0)

    def give_early():
        early[me] = (num[1, 0:FIRST, :] * gain_of(DH, FIRST)).astype(BF16)
        spread(1)

    def give_last():
        n = DH - FIRST
        last[me, :, 0:tok] = (num[1, FIRST:DH, :] * gain_of(DH + FIRST, n)).astype(BF16)
        flat = inverse_norm(1)
        scale = jnp.concatenate([flat[:, i * LANES:(i + 1) * LANES] for i in range(tok // LANES)], axis=0)
        high = scale.astype(BF16).astype(F32)
        side = jnp.concatenate([high, scale - high, jnp.zeros((n - 8, LANES), F32)], axis=0)
        last[me, :, tok:tok + LANES] = side.astype(BF16)
        each(NH, lambda i: copy_last(i).start())

    def pass_on(h):
        for i in (1, 3, 2):
            copy_n(h, i, True).wait_recv()
            copy_pair(h, i).start()

    def gathered(h):
        for i in range(NH // 2):
            copy_pair(h, i, True).wait_recv()

    def project_second(s):
        block = jnp.concatenate([early[s], last[s, :, 0:tok]], axis=0)
        side = last[s, :, tok:tok + LANES].astype(F32)
        parts = tok // LANES
        scale = side[0:parts] + side[parts:2 * parts]
        flat = jnp.concatenate([scale[i:i + 1] for i in range(parts)], axis=1)
        acc[...] += nn(wt2[s], block) * flat

    totals(0)
    totals(1)
    prefixes(0)
    totals(2)
    prefixes(1)
    totals(3)
    prefixes(2)
    each(NH, lambda i: copy_w(i, True).wait_recv())
    turned = [jnp.transpose(wbuf[s].astype(F32)) for s in range(NH)]
    wt[...] = jnp.concatenate([t[:, 0:DH] for t in turned], axis=1).astype(BF16)
    for s in range(NH):
        wt2[s] = turned[s][:, DH:].astype(BF16)
    prefixes(3)
    read_out_first(0)
    read_out_first(1)
    give_first()
    read_out_second(2)
    give_early()
    read_out_second(3)
    give_last()
    pass_on(0)
    gathered(0)
    acc[...] = nn(wt[...], jnp.concatenate([ncat[s] for s in range(NH)], axis=0))
    pass_on(1)
    gathered(1)
    project_second(me)
    for i in (1, 7, 2, 6, 3, 5, 4):
        copy_last(i, True).wait_recv()
        project_second(lax.rem(me + NH - i, NH))
    out_ref[...] = jnp.transpose(acc[...]).astype(BF16)

    for r in range(ROUNDS):
        each(NZ, lambda i: copy1(r, i).wait_send())
        def sent(i, r=r):
            @pl.when(y + i < NY)
            def _():
                copy_y(r, i).wait_send()
        each(NY, sent)
        def given(i, r=r):
            @pl.when(y + lax.rem(z + i, NZ) > 0)
            def _():
                copy2(r, i).wait_send()
        each(NZ, given)
    each(NH, lambda i: copy_w(i).wait_send())
    for h in range(2):
        each(NH // 2, lambda i: copy_n(h, i).wait_send())
        for i in range(NH // 2):
            copy_pair(h, i).wait_send()
    each(NH, lambda i: copy_last(i).wait_send())


def per_device(queries, keys, values, gain, out_weight):
    tok, width = queries.shape
    rows = max(ROWS)
    vmem = pl.BlockSpec(memory_space=pltpu.VMEM)
    dma = pltpu.SemaphoreType.DMA
    return pl.pallas_call(
        kernel,
        out_shape=jax.ShapeDtypeStruct((tok, width), BF16),
        in_specs=[pl.BlockSpec(memory_space=pltpu.HBM)] * 5,
        out_specs=vmem,
        scratch_shapes=[
            pltpu.VMEM((tok, width), BF16),
            pltpu.VMEM((tok, width), BF16),
            pltpu.VMEM((tok, width), BF16),
            pltpu.VMEM((1, width), F32),
            pltpu.VMEM(out_weight.shape, BF16),
            pltpu.VMEM((2, tok, LANES), F32),
            pltpu.VMEM((2, tok, LANES), F32),
            pltpu.VMEM((2, tok, LANES), F32),
            pltpu.VMEM((2, tok, LANES), F32),
            pltpu.VMEM((LANES, tok), BF16),
            pltpu.VMEM((2, 17, tok, LANES), BF16),
            pltpu.VMEM((2, DH, tok), F32),
            pltpu.VMEM((NH, LANES, LANES), BF16),
            pltpu.VMEM((LANES, NH * DH), BF16),
            pltpu.VMEM((NH, LANES, DH), BF16),
            pltpu.VMEM((LANES, tok), F32),
            pltpu.VMEM((DH, LANES), BF16),
            pltpu.VMEM((NH, DH, tok), BF16),
            pltpu.VMEM((NH, FIRST, tok), BF16),
            pltpu.VMEM((NH, DH - FIRST, tok + LANES), BF16),
            pltpu.VMEM((ROUNDS, NZ, rows, LANES), BF16),
            pltpu.VMEM((ROUNDS, NZ, rows, LANES), BF16),
            pltpu.VMEM((ROUNDS, NY, rows, LANES), F32),
            pltpu.VMEM((ROUNDS, NZ, rows, LANES), BF16),
            pltpu.VMEM((ROUNDS, NZ, rows, LANES), BF16),
            dma((ROUNDS, NZ)), dma((ROUNDS, NZ)),
            dma((ROUNDS, NY)), dma((ROUNDS, NY)),
            dma((ROUNDS, NZ)), dma((ROUNDS, NZ)),
            dma((NH,)), dma((NH,)),
            dma((2, NH // 2)), dma((2, NH)), dma((2, NH // 2)),
            dma((NH,)), dma((NH,)),
            dma((5,)),
        ],
        compiler_params=pltpu.CompilerParams(
            collective_id=0, has_side_effects=True, vmem_limit_bytes=55040 << 10),
    )(queries, keys, values, gain.reshape(1, width), out_weight)


def solution(mesh):
    return jax.shard_map(
        per_device,
        mesh=mesh,
        in_specs=(P("ctx", "head"), P("ctx", "head"), P("ctx", "head"), P("head"), P("head", None)),
        out_specs=P("ctx", "head"),
        check_vma=False,
    )
```

```python
import functools

import jax
import jax.numpy as jnp
from jax import lax
from jax.experimental import pallas as pl
from jax.experimental.pallas import tpu as pltpu
from jax.sharding import PartitionSpec as P

MESH = pl.DeviceIdType.MESH
DH = 64
LANES = 128
EPSILON = 1e-06
NZ = 8
NY = 4
NH = 8
ROUNDS = 4
PAIRS = NZ // 2
EXTRA = 16
F32 = jnp.float32
BF16 = jnp.bfloat16


def nt(a, b):
    return lax.dot_general(a, b, (((1,), (1,)), ((), ())), preferred_element_type=F32)


def nn(a, b):
    return lax.dot_general(a, b, (((1,), (0,)), ((), ())), preferred_element_type=F32)


FIRST = 48
ROWS = (DH + EXTRA, DH, 2 * FIRST, 2 * (DH - FIRST))


def rows_of(r):
    return ROWS[r]


def kernel(q_hbm, k_hbm, v_hbm, gain_hbm, w_hbm, out_ref,
           q_ref, k_ref, v_ref, gain_ref, w_ref, kx, kz, qx, qz, vt, qf, num, wbuf, wt, wt2, acc, middles, ncat, early, last, send1, got1, sum1, recv1, ybuf, send2, got2, sum2, recv2,
           a_send, a_recv, b_send, b_recv, y_send, y_recv, c_send, c_recv, d_send, d_recv, w_send, w_recv, n_send, n_recv, p_send, l_send, l_recv, loaded):
    ctx = lax.axis_index("ctx")
    y, z = ctx // NZ, lax.rem(ctx, NZ)
    me = lax.axis_index("head")
    pair, even = z // 2, lax.rem(z, 2) == 0
    side = 1 - 2 * lax.rem(z, 2)
    tok = q_ref.shape[0]

    def load(i):
        pairs = ((k_hbm, k_ref), (v_hbm, v_ref), (q_hbm, q_ref), (w_hbm, w_ref), (gain_hbm, gain_ref))
        return pltpu.make_async_copy(*pairs[i], loaded.at[i])

    for i in range(5):
        load(i).start()

    barrier = pltpu.get_barrier_semaphore()

    def greet(kind, count):
        def body(i, c):
            pl.semaphore_signal(barrier, inc=1, device_id=kind(i), device_id_type=MESH)
            return c
        lax.fori_loop(1, count, body, 0)

    def z_peer(i):
        return {"ctx": y * NZ + lax.rem(z + i, NZ)}

    def y_peer(i):
        return {"ctx": lax.rem(y + i, NY) * NZ + z}

    def h_peer(i):
        return {"head": lax.rem(me + i, NH)}

    greet(z_peer, NZ)
    greet(y_peer, NY)
    greet(h_peer, NH)

    lane = lax.broadcasted_iota(jnp.int32, (tok, LANES), 1)
    low = lane < DH

    def prepare(both, x_ref, z_ref):
        swapped = pltpu.roll(both, DH, 1)
        for h in range(2):
            xx = jnp.where(low, both, swapped) if h == 0 else jnp.where(low, swapped, both)
            x_ref[h] = xx
            z_ref[h] = jnp.where(low, xx, pltpu.roll(xx, DH // 2, 1))

    def products(x_ref, z_ref, h, first, count):
        fixed = z_ref[h].astype(BF16)
        turned = [pltpu.roll(x_ref[h], (LANES - d) % LANES, 1) for d in range(first, first + count)]
        return [fixed * t.astype(BF16) for t in turned]

    def middle(both, x_ref):
        shifted = jnp.where(low, pltpu.roll(x_ref[0], LANES - 16, 1), pltpu.roll(x_ref[1], LANES - 16, 1))
        return both * shifted

    load(0).wait()
    keys32 = k_ref[...].astype(F32)
    prepare(keys32, kx, kz)
    load(1).wait()
    vt[...] = jnp.transpose(v_ref[...].astype(F32)).astype(BF16)

    def toward(k):
        return lax.rem(z + side * k + 2 * NZ, NZ)

    def place(o):
        return lax.rem(side * (o - z) + 2 * NZ, NZ)

    def states(h, half):
        feats = jnp.concatenate(products(kx, kz, h, half * NZ, NZ), axis=1)
        state = nn(vt[h * DH:(h + 1) * DH, :], feats).astype(BF16)
        for o in range(NZ):
            piece = state[:, o * LANES:(o + 1) * LANES]
            if h == 0:
                send1[half, place(o), 0:DH, :] = piece
            else:
                last = DH - FIRST
                send1[2, place(o), half * FIRST:(half + 1) * FIRST, :] = piece[:FIRST]
                send1[3, place(o), half * last:(half + 1) * last, :] = piece[FIRST:]

    def extra_state():
        feats = middle(k_ref[...].astype(F32), kx).astype(BF16)
        pair = nn(vt[...], feats)
        state = jnp.where(low[:DH], pair[:DH], pair[DH:])
        for o in range(NZ):
            piece = jnp.concatenate([state[8 * o:8 * o + 8], jnp.zeros((8, LANES), F32)], axis=0)
            send1[0, place(o), DH:DH + EXTRA, :] = piece.astype(BF16)

    def columns(i):
        return pl.ds(pl.multiple_of(i * LANES, LANES), LANES)

    def copy(src, dst, sends, recvs, peer):
        return pltpu.make_async_remote_copy(
            src_ref=src, dst_ref=dst, send_sem=sends, recv_sem=recvs, device_id=peer, device_id_type=MESH)

    def at_z(i):
        return {"ctx": y * NZ + i}

    def part(ref, r, i):
        return ref.at[r, i, pl.ds(0, rows_of(r))]

    def copy_a(r):
        n = rows_of(r)
        return copy(send1.at[r, pl.ds(1, 4), pl.ds(0, n)], got1.at[r, :, pl.ds(0, n)],
                    a_send.at[r], a_recv.at[r], at_z(toward(1)))

    def copy_b(r, j):
        return copy(part(sum1, r, j - 1), part(recv1, r, pair),
                    b_send.at[r, j - 1], b_recv.at[r, pair], at_z(toward(-j)))

    def from_b(r, i):
        p = lax.rem(pair + i, PAIRS)
        return copy(part(sum1, r, i - 1), part(recv1, r, p),
                    b_send.at[r, i - 1], b_recv.at[r, p], at_z(toward(-1)))

    def gateway(j):
        return toward(2) if j == 2 else toward(-j)

    def copy_c(r, j):
        to = gateway(j)
        return copy(part(send2, r, to // 2), part(got2, r, j - 1),
                    c_send.at[r, j - 1], c_recv.at[r, j - 1], at_z(to))

    def copy_d(r, j):
        owner = toward(-j)
        return copy(part(sum2, r, j), part(recv2, r, owner),
                    d_send.at[r, j], d_recv.at[r, owner], at_z(toward(1)))

    def from_d(r, k):
        owner = toward(k)
        return copy(part(sum2, r, k - 1), part(recv2, r, owner),
                    d_send.at[r, k - 1], d_recv.at[r, owner], at_z(toward(1)))

    def needs_c(j):
        return y + gateway(j) // 2 > 0

    def needs_d():
        return jnp.logical_or(y > 0, z != 1)

    def copy_y(r, i, arriving=False):
        o, n = lax.rem(y + i, NY), rows_of(r)
        s = lax.rem(y + NY - i, NY) if arriving else y
        return copy(ybuf.at[r, y, pl.ds(0, n)], ybuf.at[r, s, pl.ds(0, n)],
                    y_send.at[r, o], y_recv.at[r, s], y_peer(i))

    def head_from(i, arriving):
        return lax.rem(me + NH - i, NH) if arriving else me

    def copy_w(i, arriving=False):
        o, s = lax.rem(me + i, NH), head_from(i, arriving)
        return copy(w_ref.at[:, columns(o)], wbuf.at[s], w_send.at[o], w_recv.at[s], h_peer(i))

    def copy_n(h, i, arriving=False):
        s, held = head_from(2 * i, arriving), (ncat, early)[h]
        return copy(held.at[me], held.at[s], n_send.at[h, i], n_recv.at[h, s], h_peer(2 * i))

    sibling = {"head": me + 1 - 2 * lax.rem(me, 2)}

    def copy_pair(h, i, arriving=False):
        mine, held = lax.rem(me + NH - 2 * i, NH), (ncat, early)[h]
        s = mine + 1 - 2 * lax.rem(me, 2) if arriving else mine
        return copy(held.at[mine], held.at[s], p_send.at[h, i], n_recv.at[h, s], sibling)

    def copy_last(i, arriving=False):
        s = head_from(i, arriving)
        return copy(last.at[me], last.at[s], l_send.at[i], l_recv.at[s], h_peer(i))

    def each(count, do):
        def body(i, c):
            do(i)
            return c
        lax.fori_loop(1, count, body, 0)

    extra_state()
    for r in range(3):
        if r < 2:
            states(0, r)
        else:
            states(1, 0)
            states(1, 1)
        if r == 0:
            pl.semaphore_wait(barrier, NZ + NY + NH - 3)
        copy_a(r).start()
        if r == 2:
            copy_a(3).start()
    load(3).wait()
    each(NH, lambda i: copy_w(i).start())
    wbuf[me] = w_ref[:, columns(me)]

    load(2).wait()
    queries32 = q_ref[...].astype(F32) * 0.125
    prepare(queries32, qx, qz)
    for h in range(2):
        mine = low if h == 0 else jnp.logical_not(low)
        qf[h, 16] = jnp.where(mine, middle(queries32 * 2.0, qx), 0.0).astype(BF16)
        qf[h, 0] = products(qx, qz, h, 0, 1)[0]
        qz[h] = qz[h] * 2.0
        for i, feats in enumerate(products(qx, qz, h, 1, 15)):
            qf[h, i + 1] = feats

    def intra(h):
        mine = low if h == 0 else jnp.logical_not(low)
        masked = jnp.where(mine, queries32, 0.0).astype(BF16)
        for b in range(2):
            seen, first = 256 * (b + 1), 256 * b
            scores = nt(k_ref[0:seen, :], masked[first:first + 256])
            s_at = lax.broadcasted_iota(jnp.int32, (seen, 256), 0)
            t_at = lax.broadcasted_iota(jnp.int32, (seen, 256), 1) + first
            weights = jnp.where(s_at <= t_at, scores * scores, 0.0).astype(BF16)
            num[h, :, first:first + 256] = nn(vt[h * DH:(h + 1) * DH, 0:seen], weights)


    def combine(r):
        n = rows_of(r)
        copy_a(r).wait_recv()
        for j in range(1, 4):
            both = send1[r, NZ - j, 0:n, :].astype(F32) + got1[r, j, 0:n, :].astype(F32)
            sum1[r, j - 1, 0:n, :] = both.astype(BF16)
            copy_b(r, j).start()

    def totals(r):
        n = rows_of(r)
        both = send1[r, 0, 0:n, :].astype(F32) + got1[r, 0, 0:n, :].astype(F32)
        recv1[r, pair, 0:n, :] = both.astype(BF16)
        for i in range(1, PAIRS):
            from_b(r, i).wait_recv()
        total = recv1[r, 0, 0:n, :].astype(F32)
        for p in range(1, PAIRS):
            total += recv1[r, p, 0:n, :].astype(F32)
        ybuf[r, y, 0:n, :] = total

        def to_later(i):
            @pl.when(y + i < NY)
            def _():
                copy_y(r, i).start()
        each(NY, to_later)

    def prefixes(r):
        n = rows_of(r)

        def from_earlier(i):
            @pl.when(y >= i)
            def _():
                copy_y(r, i, True).wait_recv()
        each(NY, from_earlier)
        running = jnp.zeros((n, LANES), F32)
        for s in range(NY):
            running += jnp.where(s < y, ybuf[r, s, 0:n, :], 0.0)
        for p in range(PAIRS):
            send2[r, p, 0:n, :] = running.astype(BF16)
            running += recv1[r, p, 0:n, :].astype(F32)
        for j in (3, 2, 1):
            @pl.when(needs_c(j))
            def _(j=j):
                copy_c(r, j).start()
        share(r, 0, z, send2[r, pair, 0:n, :], send1[r, 0, 0:n, :], got1[r, 0, 0:n, :])

    def share(r, j, owner, before, mine, other):
        n = rows_of(r)
        after = (before.astype(F32) + jnp.where(even, mine, other).astype(F32)).astype(BF16)
        recv2[r, owner, 0:n, :] = jnp.where(even, before, after)
        sum2[r, j, 0:n, :] = jnp.where(even, after, before)

        @pl.when(needs_d())
        def _():
            copy_d(r, j).start()

    def relay(r):
        n = rows_of(r)

        @pl.when(y + pair > 0)
        def _():
            for j in range(1, 4):
                copy_c(r, j).wait_recv()

        @pl.when(y + pair == 0)
        def _():
            got2[r] = jnp.zeros(got2.shape[1:], BF16)

        for j in range(1, 4):
            share(r, j, toward(-j), got2[r, j - 1, 0:n, :], send1[r, NZ - j, 0:n, :], got1[r, j, 0:n, :])

    def arrived(r):
        @pl.when(y + z > 0)
        def _():
            for k in range(1, 5):
                from_d(r, k).wait_recv()

        @pl.when(y + z == 0)
        def _():
            recv2[r] = jnp.zeros(recv2.shape[1:], BF16)

    def read_out_first(half):
        arrived(half)
        prefix = [recv2[half, o, 0:DH, :] for o in range(NZ)]
        feats = [qf[0, half * NZ + o] for o in range(NZ)]
        if half == 0:
            pieces = [recv2[0, o, DH:DH + EXTRA, :].astype(F32)[:8] for o in range(NZ)]
            middles[...] = jnp.concatenate(pieces, axis=0).astype(BF16)
            prefix.append(middles[...])
            feats.append(qf[0, 16])
        num[0] += nt(jnp.concatenate(prefix, axis=1), jnp.concatenate(feats, axis=1))

    def read_out_second(r):
        first, n = (0, FIRST) if r == 2 else (FIRST, DH - FIRST)
        arrived(r)
        prefix = [recv2[r, o, half * n:(half + 1) * n, :] for half in range(2) for o in range(NZ)]
        prefix.append(middles[first:first + n, :])
        feats = [qf[1, i] for i in range(17)]
        num[1, first:first + n, :] += nt(jnp.concatenate(prefix, axis=1), jnp.concatenate(feats, axis=1))

    load(4).wait()
    gains = jnp.transpose(jnp.broadcast_to(gain_ref[...], (LANES, LANES)))

    def gain_of(first, n):
        return jnp.concatenate([gains[first:first + n]] * (tok // LANES), axis=1)

    def inverse_norm(h):
        value = num[h]
        return lax.rsqrt(jnp.mean(value * value, axis=0, keepdims=True) + EPSILON)

    def spread(h):
        each(NH // 2, lambda i: copy_n(h, i).start())
        copy_pair(h, 0).start()

    def give_first():
        ncat[me] = (num[0] * inverse_norm(0) * gain_of(0, DH)).astype(BF16)
        spread(0)

    def give_early():
        early[me] = (num[1, 0:FIRST, :] * gain_of(DH, FIRST)).astype(BF16)
        spread(1)

    def give_last():
        n = DH - FIRST
        last[me, :, 0:tok] = (num[1, FIRST:DH, :] * gain_of(DH + FIRST, n)).astype(BF16)
        flat = inverse_norm(1)
        scale = jnp.concatenate([flat[:, i * LANES:(i + 1) * LANES] for i in range(tok // LANES)], axis=0)
        high = scale.astype(BF16).astype(F32)
        side = jnp.concatenate([high, scale - high, jnp.zeros((n - 8, LANES), F32)], axis=0)
        last[me, :, tok:tok + LANES] = side.astype(BF16)
        each(NH, lambda i: copy_last(i).start())

    def pass_on(h):
        for i in (1, 3, 2):
            copy_n(h, i, True).wait_recv()
            copy_pair(h, i).start()

    def gathered(h):
        for i in range(NH // 2):
            copy_pair(h, i, True).wait_recv()

    def project_second(s):
        block = jnp.concatenate([early[s], last[s, :, 0:tok]], axis=0)
        side = last[s, :, tok:tok + LANES].astype(F32)
        parts = tok // LANES
        scale = side[0:parts] + side[parts:2 * parts]
        flat = jnp.concatenate([scale[i:i + 1] for i in range(parts)], axis=1)
        acc[...] += nn(wt2[s], block) * flat

    combine(0)
    intra(0)
    combine(1)
    intra(1)
    combine(2)
    combine(3)
    each(NH, lambda i: copy_w(i, True).wait_recv())
    turned = [jnp.transpose(wbuf[s].astype(F32)) for s in range(NH)]
    wt[...] = jnp.concatenate([t[:, 0:DH] for t in turned], axis=1).astype(BF16)
    for s in range(NH):
        wt2[s] = turned[s][:, DH:].astype(BF16)
    totals(0)
    totals(1)
    totals(2)
    prefixes(0)
    totals(3)
    for r in range(1, ROUNDS):
        prefixes(r)
    for r in range(ROUNDS):
        relay(r)
    read_out_first(0)
    read_out_first(1)
    give_first()
    read_out_second(2)
    give_early()
    read_out_second(3)
    give_last()
    pass_on(0)
    gathered(0)
    acc[...] = nn(wt[...], jnp.concatenate([ncat[s] for s in range(NH)], axis=0))
    pass_on(1)
    gathered(1)
    project_second(me)
    for i in (1, 7, 2, 6, 3, 5, 4):
        copy_last(i, True).wait_recv()
        project_second(lax.rem(me + NH - i, NH))
    out_ref[...] = jnp.transpose(acc[...]).astype(BF16)

    for r in range(ROUNDS):
        copy_a(r).wait_send()

        def sent(i, r=r):
            @pl.when(y + i < NY)
            def _():
                copy_y(r, i).wait_send()
        each(NY, sent)
        for j in range(1, 4):
            copy_b(r, j).wait_send()

            @pl.when(needs_c(j))
            def _(r=r, j=j):
                copy_c(r, j).wait_send()

        @pl.when(needs_d())
        def _(r=r):
            for j in range(4):
                copy_d(r, j).wait_send()
    each(NH, lambda i: copy_w(i).wait_send())
    for h in range(2):
        each(NH // 2, lambda i: copy_n(h, i).wait_send())
        for i in range(NH // 2):
            copy_pair(h, i).wait_send()
    each(NH, lambda i: copy_last(i).wait_send())


def per_device(queries, keys, values, gain, out_weight):
    tok, width = queries.shape
    rows = max(ROWS)
    vmem = pl.BlockSpec(memory_space=pltpu.VMEM)
    dma = pltpu.SemaphoreType.DMA
    return pl.pallas_call(
        kernel,
        out_shape=jax.ShapeDtypeStruct((tok, width), BF16),
        in_specs=[pl.BlockSpec(memory_space=pltpu.HBM)] * 5,
        out_specs=vmem,
        scratch_shapes=[
            pltpu.VMEM((tok, width), BF16),
            pltpu.VMEM((tok, width), BF16),
            pltpu.VMEM((tok, width), BF16),
            pltpu.VMEM((1, width), F32),
            pltpu.VMEM(out_weight.shape, BF16),
            pltpu.VMEM((2, tok, LANES), F32),
            pltpu.VMEM((2, tok, LANES), F32),
            pltpu.VMEM((2, tok, LANES), F32),
            pltpu.VMEM((2, tok, LANES), F32),
            pltpu.VMEM((LANES, tok), BF16),
            pltpu.VMEM((2, 17, tok, LANES), BF16),
            pltpu.VMEM((2, DH, tok), F32),
            pltpu.VMEM((NH, LANES, LANES), BF16),
            pltpu.VMEM((LANES, NH * DH), BF16),
            pltpu.VMEM((NH, LANES, DH), BF16),
            pltpu.VMEM((LANES, tok), F32),
            pltpu.VMEM((DH, LANES), BF16),
            pltpu.VMEM((NH, DH, tok), BF16),
            pltpu.VMEM((NH, FIRST, tok), BF16),
            pltpu.VMEM((NH, DH - FIRST, tok + LANES), BF16),
            pltpu.VMEM((ROUNDS, NZ, rows, LANES), BF16),
            pltpu.VMEM((ROUNDS, 4, rows, LANES), BF16),
            pltpu.VMEM((ROUNDS, 3, rows, LANES), BF16),
            pltpu.VMEM((ROUNDS, PAIRS, rows, LANES), BF16),
            pltpu.VMEM((ROUNDS, NY, rows, LANES), F32),
            pltpu.VMEM((ROUNDS, PAIRS, rows, LANES), BF16),
            pltpu.VMEM((ROUNDS, 3, rows, LANES), BF16),
            pltpu.VMEM((ROUNDS, 4, rows, LANES), BF16),
            pltpu.VMEM((ROUNDS, NZ, rows, LANES), BF16),
            dma((ROUNDS,)), dma((ROUNDS,)),
            dma((ROUNDS, 3)), dma((ROUNDS, PAIRS)),
            dma((ROUNDS, NY)), dma((ROUNDS, NY)),
            dma((ROUNDS, 3)), dma((ROUNDS, 3)),
            dma((ROUNDS, 4)), dma((ROUNDS, NZ)),
            dma((NH,)), dma((NH,)),
            dma((2, NH // 2)), dma((2, NH)), dma((2, NH // 2)),
            dma((NH,)), dma((NH,)),
            dma((5,)),
        ],
        compiler_params=pltpu.CompilerParams(
            collective_id=0, has_side_effects=True, vmem_limit_bytes=55040 << 10),
    )(queries, keys, values, gain.reshape(1, width), out_weight)


def solution(mesh):
    return jax.shard_map(
        per_device,
        mesh=mesh,
        in_specs=(P("ctx", "head"), P("ctx", "head"), P("ctx", "head"), P("head"), P("head", None)),
        out_specs=P("ctx", "head"),
        check_vma=False,
    )
```

```python
import functools

import jax
import jax.numpy as jnp
from jax import lax
from jax.experimental import pallas as pl
from jax.experimental.pallas import tpu as pltpu
from jax.sharding import PartitionSpec as P

MESH = pl.DeviceIdType.MESH
DH = 64
LANES = 128
EPSILON = 1e-06
NZ = 8
NY = 4
NH = 8
ROUNDS = 4
PAIRS = NZ // 2
EXTRA = 16
F32 = jnp.float32
BF16 = jnp.bfloat16


def nt(a, b):
    return lax.dot_general(a, b, (((1,), (1,)), ((), ())), preferred_element_type=F32)


def nn(a, b):
    return lax.dot_general(a, b, (((1,), (0,)), ((), ())), preferred_element_type=F32)


FIRST = 48
ROWS = (DH + EXTRA, DH, 2 * FIRST, 2 * (DH - FIRST))


def rows_of(r):
    return ROWS[r]


def kernel(q_hbm, k_hbm, v_hbm, gain_hbm, w_hbm, out_ref,
           q_ref, k_ref, v_ref, gain_ref, w_ref, kx, kz, qx, qz, vt, qf, num, wbuf, wt, wt2, acc, middles, ncat, early, last, send1, got1, sum1, recv1, ybuf, send2, got2, sum2, recv2,
           a_send, a_recv, b_send, b_recv, y_send, y_recv, c_send, c_recv, d_send, d_recv, w_send, w_recv, n_send, n_recv, p_send, l_send, l_recv, loaded):
    ctx = lax.axis_index("ctx")
    y, z = ctx // NZ, lax.rem(ctx, NZ)
    me = lax.axis_index("head")
    pair, even = z // 2, lax.rem(z, 2) == 0
    side = 1 - 2 * lax.rem(z, 2)
    tok = q_ref.shape[0]

    def load(i):
        pairs = ((k_hbm, k_ref), (v_hbm, v_ref), (q_hbm, q_ref), (w_hbm, w_ref), (gain_hbm, gain_ref))
        return pltpu.make_async_copy(*pairs[i], loaded.at[i])

    for i in range(5):
        load(i).start()

    barrier = pltpu.get_barrier_semaphore()

    def greet(kind, count):
        def body(i, c):
            pl.semaphore_signal(barrier, inc=1, device_id=kind(i), device_id_type=MESH)
            return c
        lax.fori_loop(1, count, body, 0)

    def z_peer(i):
        return {"ctx": y * NZ + lax.rem(z + i, NZ)}

    def y_peer(i):
        return {"ctx": lax.rem(y + i, NY) * NZ + z}

    def h_peer(i):
        return {"head": lax.rem(me + i, NH)}

    greet(z_peer, NZ)
    greet(y_peer, NY)
    greet(h_peer, NH)

    lane = lax.broadcasted_iota(jnp.int32, (tok, LANES), 1)
    low = lane < DH

    def prepare(both, x_ref, z_ref):
        swapped = pltpu.roll(both, DH, 1)
        for h in range(2):
            xx = jnp.where(low, both, swapped) if h == 0 else jnp.where(low, swapped, both)
            x_ref[h] = xx
            z_ref[h] = jnp.where(low, xx, pltpu.roll(xx, DH // 2, 1))

    def products(x_ref, z_ref, h, first, count):
        fixed = z_ref[h].astype(BF16)
        turned = [pltpu.roll(x_ref[h], (LANES - d) % LANES, 1) for d in range(first, first + count)]
        return [fixed * t.astype(BF16) for t in turned]

    def middle(both, x_ref):
        shifted = jnp.where(low, pltpu.roll(x_ref[0], LANES - 16, 1), pltpu.roll(x_ref[1], LANES - 16, 1))
        return both * shifted

    load(0).wait()
    keys32 = k_ref[...].astype(F32)
    prepare(keys32, kx, kz)
    load(1).wait()
    vt[...] = jnp.transpose(v_ref[...].astype(F32)).astype(BF16)

    def toward(k):
        return lax.rem(z + side * k + 2 * NZ, NZ)

    def place(o):
        return lax.rem(side * (o - z) + 2 * NZ, NZ)

    def states(h, half):
        feats = jnp.concatenate(products(kx, kz, h, half * NZ, NZ), axis=1)
        state = nn(vt[h * DH:(h + 1) * DH, :], feats).astype(BF16)
        for o in range(NZ):
            piece = state[:, o * LANES:(o + 1) * LANES]
            if h == 0:
                send1[half, place(o), 0:DH, :] = piece
            else:
                last = DH - FIRST
                send1[2, place(o), half * FIRST:(half + 1) * FIRST, :] = piece[:FIRST]
                send1[3, place(o), half * last:(half + 1) * last, :] = piece[FIRST:]

    def extra_state():
        feats = middle(k_ref[...].astype(F32), kx).astype(BF16)
        pair = nn(vt[...], feats)
        state = jnp.where(low[:DH], pair[:DH], pair[DH:])
        for o in range(NZ):
            piece = jnp.concatenate([state[8 * o:8 * o + 8], jnp.zeros((8, LANES), F32)], axis=0)
            send1[0, place(o), DH:DH + EXTRA, :] = piece.astype(BF16)

    def columns(i):
        return pl.ds(pl.multiple_of(i * LANES, LANES), LANES)

    def copy(src, dst, sends, recvs, peer):
        return pltpu.make_async_remote_copy(
            src_ref=src, dst_ref=dst, send_sem=sends, recv_sem=recvs, device_id=peer, device_id_type=MESH)

    def at_z(i):
        return {"ctx": y * NZ + i}

    def part(ref, r, i):
        return ref.at[r, i, pl.ds(0, rows_of(r))]

    def copy_a(r):
        n = rows_of(r)
        return copy(send1.at[r, pl.ds(1, 4), pl.ds(0, n)], got1.at[r, :, pl.ds(0, n)],
                    a_send.at[r], a_recv.at[r], at_z(toward(1)))

    def copy_b(r, j):
        return copy(part(sum1, r, j - 1), part(recv1, r, pair),
                    b_send.at[r, j - 1], b_recv.at[r, pair], at_z(toward(-j)))

    def from_b(r, i):
        p = lax.rem(pair + i, PAIRS)
        return copy(part(sum1, r, i - 1), part(recv1, r, p),
                    b_send.at[r, i - 1], b_recv.at[r, p], at_z(toward(-1)))

    def gateway(j):
        return toward(2) if j == 2 else toward(-j)

    def copy_c(r, j):
        to = gateway(j)
        return copy(part(send2, r, to // 2), part(got2, r, j - 1),
                    c_send.at[r, j - 1], c_recv.at[r, j - 1], at_z(to))

    def copy_d(r, j):
        owner = toward(-j)
        return copy(part(sum2, r, j), part(recv2, r, owner),
                    d_send.at[r, j], d_recv.at[r, owner], at_z(toward(1)))

    def from_d(r, k):
        owner = toward(k)
        return copy(part(sum2, r, k - 1), part(recv2, r, owner),
                    d_send.at[r, k - 1], d_recv.at[r, owner], at_z(toward(1)))

    def needs_c(j):
        return y + gateway(j) // 2 > 0

    def needs_d():
        return jnp.logical_or(y > 0, z != 1)

    def copy_y(r, i, arriving=False):
        o, n = lax.rem(y + i, NY), rows_of(r)
        s = lax.rem(y + NY - i, NY) if arriving else y
        return copy(ybuf.at[r, y, pl.ds(0, n)], ybuf.at[r, s, pl.ds(0, n)],
                    y_send.at[r, o], y_recv.at[r, s], y_peer(i))

    def head_from(i, arriving):
        return lax.rem(me + NH - i, NH) if arriving else me

    def copy_w(i, arriving=False):
        o, s = lax.rem(me + i, NH), head_from(i, arriving)
        return copy(w_ref.at[:, columns(o)], wbuf.at[s], w_send.at[o], w_recv.at[s], h_peer(i))

    def copy_n(h, i, arriving=False):
        s, held = head_from(2 * i, arriving), (ncat, early)[h]
        return copy(held.at[me], held.at[s], n_send.at[h, i], n_recv.at[h, s], h_peer(2 * i))

    sibling = {"head": me + 1 - 2 * lax.rem(me, 2)}

    def copy_pair(h, i, arriving=False):
        mine, held = lax.rem(me + NH - 2 * i, NH), (ncat, early)[h]
        s = mine + 1 - 2 * lax.rem(me, 2) if arriving else mine
        return copy(held.at[mine], held.at[s], p_send.at[h, i], n_recv.at[h, s], sibling)

    def copy_last(i, arriving=False):
        s = head_from(i, arriving)
        return copy(last.at[me], last.at[s], l_send.at[i], l_recv.at[s], h_peer(i))

    def each(count, do):
        def body(i, c):
            do(i)
            return c
        lax.fori_loop(1, count, body, 0)

    extra_state()
    for r in range(3):
        if r < 2:
            states(0, r)
        else:
            states(1, 0)
            states(1, 1)
        if r == 0:
            pl.semaphore_wait(barrier, NZ + NY + NH - 3)
        copy_a(r).start()
        if r == 2:
            copy_a(3).start()
    load(3).wait()
    each(NH, lambda i: copy_w(i).start())
    wbuf[me] = w_ref[:, columns(me)]

    load(2).wait()
    queries32 = q_ref[...].astype(F32) * 0.125
    prepare(queries32, qx, qz)
    for h in range(2):
        mine = low if h == 0 else jnp.logical_not(low)
        qf[h, 16] = jnp.where(mine, middle(queries32 * 2.0, qx), 0.0).astype(BF16)
        qf[h, 0] = products(qx, qz, h, 0, 1)[0]
        qz[h] = qz[h] * 2.0
        for i, feats in enumerate(products(qx, qz, h, 1, 15)):
            qf[h, i + 1] = feats

    def intra(h):
        mine = low if h == 0 else jnp.logical_not(low)
        masked = jnp.where(mine, queries32, 0.0).astype(BF16)
        for b in range(2):
            seen, first = 256 * (b + 1), 256 * b
            scores = nt(k_ref[0:seen, :], masked[first:first + 256])
            s_at = lax.broadcasted_iota(jnp.int32, (seen, 256), 0)
            t_at = lax.broadcasted_iota(jnp.int32, (seen, 256), 1) + first
            weights = jnp.where(s_at <= t_at, scores * scores, 0.0).astype(BF16)
            num[h, :, first:first + 256] = nn(vt[h * DH:(h + 1) * DH, 0:seen], weights)


    def combine(r):
        n = rows_of(r)
        copy_a(r).wait_recv()
        for j in (3, 2, 1):
            both = send1[r, NZ - j, 0:n, :].astype(F32) + got1[r, j, 0:n, :].astype(F32)
            sum1[r, j - 1, 0:n, :] = both.astype(BF16)
            copy_b(r, j).start()

    def totals(r):
        n = rows_of(r)
        both = send1[r, 0, 0:n, :].astype(F32) + got1[r, 0, 0:n, :].astype(F32)
        recv1[r, pair, 0:n, :] = both.astype(BF16)
        for i in range(1, PAIRS):
            from_b(r, i).wait_recv()
        total = recv1[r, 0, 0:n, :].astype(F32)
        for p in range(1, PAIRS):
            total += recv1[r, p, 0:n, :].astype(F32)
        ybuf[r, y, 0:n, :] = total.astype(BF16)

        def to_later(i):
            @pl.when(y + i < NY)
            def _():
                copy_y(r, i).start()
        each(NY, to_later)

    def prefixes(r):
        n = rows_of(r)

        def from_earlier(i):
            @pl.when(y >= i)
            def _():
                copy_y(r, i, True).wait_recv()
        each(NY, from_earlier)
        running = jnp.zeros((n, LANES), F32)
        for s in range(NY):
            running += jnp.where(s < y, ybuf[r, s, 0:n, :].astype(F32), 0.0)
        for p in range(PAIRS):
            send2[r, p, 0:n, :] = running.astype(BF16)
            running += recv1[r, p, 0:n, :].astype(F32)
        for j in (3, 2, 1):
            @pl.when(needs_c(j))
            def _(j=j):
                copy_c(r, j).start()
        share(r, 0, z, send2[r, pair, 0:n, :], send1[r, 0, 0:n, :], got1[r, 0, 0:n, :])

    def share(r, j, owner, before, mine, other):
        n = rows_of(r)
        after = (before.astype(F32) + jnp.where(even, mine, other).astype(F32)).astype(BF16)
        recv2[r, owner, 0:n, :] = jnp.where(even, before, after)
        sum2[r, j, 0:n, :] = jnp.where(even, after, before)

        @pl.when(needs_d())
        def _():
            copy_d(r, j).start()

    def relay(r):
        n = rows_of(r)

        @pl.when(y + pair == 0)
        def _():
            got2[r] = jnp.zeros(got2.shape[1:], BF16)

        for j in range(1, 4):
            @pl.when(y + pair > 0)
            def _(j=j):
                copy_c(r, j).wait_recv()
            share(r, j, toward(-j), got2[r, j - 1, 0:n, :], send1[r, NZ - j, 0:n, :], got1[r, j, 0:n, :])

    def arrived(r):
        @pl.when(y + z > 0)
        def _():
            for k in range(1, 5):
                from_d(r, k).wait_recv()

        @pl.when(y + z == 0)
        def _():
            recv2[r] = jnp.zeros(recv2.shape[1:], BF16)

    def read_out_first(half):
        arrived(half)
        prefix = [recv2[half, o, 0:DH, :] for o in range(NZ)]
        feats = [qf[0, half * NZ + o] for o in range(NZ)]
        if half == 0:
            pieces = [recv2[0, o, DH:DH + EXTRA, :].astype(F32)[:8] for o in range(NZ)]
            middles[...] = jnp.concatenate(pieces, axis=0).astype(BF16)
            prefix.append(middles[...])
            feats.append(qf[0, 16])
        num[0] += nt(jnp.concatenate(prefix, axis=1), jnp.concatenate(feats, axis=1))

    def read_out_second(r):
        first, n = (0, FIRST) if r == 2 else (FIRST, DH - FIRST)
        arrived(r)
        prefix = [recv2[r, o, half * n:(half + 1) * n, :] for half in range(2) for o in range(NZ)]
        prefix.append(middles[first:first + n, :])
        feats = [qf[1, i] for i in range(17)]
        num[1, first:first + n, :] += nt(jnp.concatenate(prefix, axis=1), jnp.concatenate(feats, axis=1))

    load(4).wait()
    gains = jnp.transpose(jnp.broadcast_to(gain_ref[...], (LANES, LANES)))

    def gain_of(first, n):
        return jnp.concatenate([gains[first:first + n]] * (tok // LANES), axis=1)

    def inverse_norm(h):
        value = num[h]
        return lax.rsqrt(jnp.mean(value * value, axis=0, keepdims=True) + EPSILON)

    def spread(h):
        for i in (2, 1, 3):
            copy_n(h, i).start()
        copy_pair(h, 0).start()

    def give_first():
        ncat[me] = (num[0] * inverse_norm(0) * gain_of(0, DH)).astype(BF16)
        spread(0)

    def give_early():
        early[me] = (num[1, 0:FIRST, :] * gain_of(DH, FIRST)).astype(BF16)
        spread(1)

    def give_last():
        n = DH - FIRST
        last[me, :, 0:tok] = (num[1, FIRST:DH, :] * gain_of(DH + FIRST, n)).astype(BF16)
        flat = inverse_norm(1)
        scale = jnp.concatenate([flat[:, i * LANES:(i + 1) * LANES] for i in range(tok // LANES)], axis=0)
        high = scale.astype(BF16).astype(F32)
        side = jnp.concatenate([high, scale - high, jnp.zeros((n - 8, LANES), F32)], axis=0)
        last[me, :, tok:tok + LANES] = side.astype(BF16)
        for i in (4, 3, 5, 2, 6, 1, 7):
            copy_last(i).start()

    def pass_on(h):
        for i in (1, 3, 2):
            copy_n(h, i, True).wait_recv()
            copy_pair(h, i).start()

    def gathered(h):
        for i in range(NH // 2):
            copy_pair(h, i, True).wait_recv()

    def project_second(s):
        block = jnp.concatenate([early[s], last[s, :, 0:tok]], axis=0)
        side = last[s, :, tok:tok + LANES].astype(F32)
        parts = tok // LANES
        scale = side[0:parts] + side[parts:2 * parts]
        flat = jnp.concatenate([scale[i:i + 1] for i in range(parts)], axis=1)
        acc[...] += nn(wt2[s], block) * flat

    combine(0)
    intra(0)
    combine(1)
    intra(1)
    combine(2)
    combine(3)
    each(NH, lambda i: copy_w(i, True).wait_recv())
    turned = [jnp.transpose(wbuf[s].astype(F32)) for s in range(NH)]
    wt[...] = jnp.concatenate([t[:, 0:DH] for t in turned], axis=1).astype(BF16)
    for s in range(NH):
        wt2[s] = turned[s][:, DH:].astype(BF16)
    for r in range(ROUNDS):
        totals(r)
    for r in range(ROUNDS):
        prefixes(r)
    for r in range(ROUNDS):
        relay(r)
    read_out_first(0)
    read_out_first(1)
    give_first()
    read_out_second(2)
    give_early()
    read_out_second(3)
    give_last()
    pass_on(0)
    gathered(0)
    acc[...] = nn(wt[...], jnp.concatenate([ncat[s] for s in range(NH)], axis=0))
    pass_on(1)
    gathered(1)
    project_second(me)
    for i in (1, 7, 2, 6, 3, 5, 4):
        copy_last(i, True).wait_recv()
        project_second(lax.rem(me + NH - i, NH))
    out_ref[...] = jnp.transpose(acc[...]).astype(BF16)

    for r in range(ROUNDS):
        copy_a(r).wait_send()

        def sent(i, r=r):
            @pl.when(y + i < NY)
            def _():
                copy_y(r, i).wait_send()
        each(NY, sent)
        for j in range(1, 4):
            copy_b(r, j).wait_send()

            @pl.when(needs_c(j))
            def _(r=r, j=j):
                copy_c(r, j).wait_send()

        @pl.when(needs_d())
        def _(r=r):
            for j in range(4):
                copy_d(r, j).wait_send()
    each(NH, lambda i: copy_w(i).wait_send())
    for h in range(2):
        each(NH // 2, lambda i: copy_n(h, i).wait_send())
        for i in range(NH // 2):
            copy_pair(h, i).wait_send()
    each(NH, lambda i: copy_last(i).wait_send())


def per_device(queries, keys, values, gain, out_weight):
    tok, width = queries.shape
    rows = max(ROWS)
    vmem = pl.BlockSpec(memory_space=pltpu.VMEM)
    dma = pltpu.SemaphoreType.DMA
    return pl.pallas_call(
        kernel,
        out_shape=jax.ShapeDtypeStruct((tok, width), BF16),
        in_specs=[pl.BlockSpec(memory_space=pltpu.HBM)] * 5,
        out_specs=vmem,
        scratch_shapes=[
            pltpu.VMEM((tok, width), BF16),
            pltpu.VMEM((tok, width), BF16),
            pltpu.VMEM((tok, width), BF16),
            pltpu.VMEM((1, width), F32),
            pltpu.VMEM(out_weight.shape, BF16),
            pltpu.VMEM((2, tok, LANES), F32),
            pltpu.VMEM((2, tok, LANES), F32),
            pltpu.VMEM((2, tok, LANES), F32),
            pltpu.VMEM((2, tok, LANES), F32),
            pltpu.VMEM((LANES, tok), BF16),
            pltpu.VMEM((2, 17, tok, LANES), BF16),
            pltpu.VMEM((2, DH, tok), F32),
            pltpu.VMEM((NH, LANES, LANES), BF16),
            pltpu.VMEM((LANES, NH * DH), BF16),
            pltpu.VMEM((NH, LANES, DH), BF16),
            pltpu.VMEM((LANES, tok), F32),
            pltpu.VMEM((DH, LANES), BF16),
            pltpu.VMEM((NH, DH, tok), BF16),
            pltpu.VMEM((NH, FIRST, tok), BF16),
            pltpu.VMEM((NH, DH - FIRST, tok + LANES), BF16),
            pltpu.VMEM((ROUNDS, NZ, rows, LANES), BF16),
            pltpu.VMEM((ROUNDS, 4, rows, LANES), BF16),
            pltpu.VMEM((ROUNDS, 3, rows, LANES), BF16),
            pltpu.VMEM((ROUNDS, PAIRS, rows, LANES), BF16),
            pltpu.VMEM((ROUNDS, NY, rows, LANES), BF16),
            pltpu.VMEM((ROUNDS, PAIRS, rows, LANES), BF16),
            pltpu.VMEM((ROUNDS, 3, rows, LANES), BF16),
            pltpu.VMEM((ROUNDS, 4, rows, LANES), BF16),
            pltpu.VMEM((ROUNDS, NZ, rows, LANES), BF16),
            dma((ROUNDS,)), dma((ROUNDS,)),
            dma((ROUNDS, 3)), dma((ROUNDS, PAIRS)),
            dma((ROUNDS, NY)), dma((ROUNDS, NY)),
            dma((ROUNDS, 3)), dma((ROUNDS, 3)),
            dma((ROUNDS, 4)), dma((ROUNDS, NZ)),
            dma((NH,)), dma((NH,)),
            dma((2, NH // 2)), dma((2, NH)), dma((2, NH // 2)),
            dma((NH,)), dma((NH,)),
            dma((5,)),
        ],
        compiler_params=pltpu.CompilerParams(
            collective_id=0, has_side_effects=True, vmem_limit_bytes=55040 << 10),
    )(queries, keys, values, gain.reshape(1, width), out_weight)


def solution(mesh):
    return jax.shard_map(
        per_device,
        mesh=mesh,
        in_specs=(P("ctx", "head"), P("ctx", "head"), P("ctx", "head"), P("head"), P("head", None)),
        out_specs=P("ctx", "head"),
        check_vma=False,
    )
```

```python
import functools

import jax
import jax.numpy as jnp
from jax import lax
from jax.experimental import pallas as pl
from jax.experimental.pallas import tpu as pltpu
from jax.sharding import PartitionSpec as P

MESH = pl.DeviceIdType.MESH
DH = 64
LANES = 128
EPSILON = 1e-06
NZ = 8
NY = 4
NH = 8
ROUNDS = 4
PAIRS = NZ // 2
EXTRA = 16
F32 = jnp.float32
BF16 = jnp.bfloat16


def nt(a, b):
    return lax.dot_general(a, b, (((1,), (1,)), ((), ())), preferred_element_type=F32)


def nn(a, b):
    return lax.dot_general(a, b, (((1,), (0,)), ((), ())), preferred_element_type=F32)


FIRST = 48
ROWS = (DH + EXTRA, DH, 2 * FIRST, 2 * (DH - FIRST))


def rows_of(r):
    return ROWS[r]


def kernel(q_hbm, k_hbm, v_hbm, gain_hbm, w_hbm, out_ref,
           q_ref, k_ref, v_ref, gain_ref, w_ref, kx, kz, qx, qz, vt, qf, num, wbuf, wt, wt2, acc, middles, ncat, early, last, send1, got1, sum1, recv1, ybuf, send2, got2, sum2, recv2,
           a_send, a_recv, b_send, b_recv, y_send, y_recv, c_send, c_recv, d_send, d_recv, w_send, w_recv, n_send, n_recv, p_send, loaded):
    ctx = lax.axis_index("ctx")
    y, z = ctx // NZ, lax.rem(ctx, NZ)
    me = lax.axis_index("head")
    pair, even = z // 2, lax.rem(z, 2) == 0
    side = 1 - 2 * lax.rem(z, 2)
    tok = q_ref.shape[0]

    def load(i):
        pairs = ((k_hbm, k_ref), (v_hbm, v_ref), (q_hbm, q_ref), (w_hbm, w_ref), (gain_hbm, gain_ref))
        return pltpu.make_async_copy(*pairs[i], loaded.at[i])

    for i in range(5):
        load(i).start()

    barrier = pltpu.get_barrier_semaphore()

    def greet(kind, count):
        def body(i, c):
            pl.semaphore_signal(barrier, inc=1, device_id=kind(i), device_id_type=MESH)
            return c
        lax.fori_loop(1, count, body, 0)

    def z_peer(i):
        return {"ctx": y * NZ + lax.rem(z + i, NZ)}

    def y_peer(i):
        return {"ctx": lax.rem(y + i, NY) * NZ + z}

    def h_peer(i):
        return {"head": lax.rem(me + i, NH)}

    greet(z_peer, NZ)
    greet(y_peer, NY)
    greet(h_peer, NH)

    lane = lax.broadcasted_iota(jnp.int32, (tok, LANES), 1)
    low = lane < DH

    def prepare(both, x_ref, z_ref):
        swapped = pltpu.roll(both, DH, 1)
        for h in range(2):
            xx = jnp.where(low, both, swapped) if h == 0 else jnp.where(low, swapped, both)
            x_ref[h] = xx
            z_ref[h] = jnp.where(low, xx, pltpu.roll(xx, DH // 2, 1))

    def products(x_ref, z_ref, h, first, count):
        fixed = z_ref[h].astype(BF16)
        turned = [pltpu.roll(x_ref[h], (LANES - d) % LANES, 1) for d in range(first, first + count)]
        return [fixed * t.astype(BF16) for t in turned]

    def middle(both, x_ref):
        shifted = jnp.where(low, pltpu.roll(x_ref[0], LANES - 16, 1), pltpu.roll(x_ref[1], LANES - 16, 1))
        return both * shifted

    load(0).wait()
    keys32 = k_ref[...].astype(F32)
    prepare(keys32, kx, kz)
    load(1).wait()
    vt[...] = jnp.transpose(v_ref[...].astype(F32)).astype(BF16)

    def toward(k):
        return lax.rem(z + side * k + 2 * NZ, NZ)

    def place(o):
        return lax.rem(side * (o - z) + 2 * NZ, NZ)

    def states(h, half):
        feats = jnp.concatenate(products(kx, kz, h, half * NZ, NZ), axis=1)
        state = nn(vt[h * DH:(h + 1) * DH, :], feats).astype(BF16)
        for o in range(NZ):
            piece = state[:, o * LANES:(o + 1) * LANES]
            if h == 0:
                send1[half, place(o), 0:DH, :] = piece
            else:
                last = DH - FIRST
                send1[2, place(o), half * FIRST:(half + 1) * FIRST, :] = piece[:FIRST]
                send1[3, place(o), half * last:(half + 1) * last, :] = piece[FIRST:]

    def extra_state():
        feats = middle(k_ref[...].astype(F32), kx).astype(BF16)
        pair = nn(vt[...], feats)
        state = jnp.where(low[:DH], pair[:DH], pair[DH:])
        for o in range(NZ):
            piece = jnp.concatenate([state[8 * o:8 * o + 8], jnp.zeros((8, LANES), F32)], axis=0)
            send1[0, place(o), DH:DH + EXTRA, :] = piece.astype(BF16)

    def columns(i):
        return pl.ds(pl.multiple_of(i * LANES, LANES), LANES)

    def copy(src, dst, sends, recvs, peer):
        return pltpu.make_async_remote_copy(
            src_ref=src, dst_ref=dst, send_sem=sends, recv_sem=recvs, device_id=peer, device_id_type=MESH)

    def at_z(i):
        return {"ctx": y * NZ + i}

    def part(ref, r, i):
        return ref.at[r, i, pl.ds(0, rows_of(r))]

    def copy_a(r):
        n = rows_of(r)
        return copy(send1.at[r, pl.ds(1, 4), pl.ds(0, n)], got1.at[r, :, pl.ds(0, n)],
                    a_send.at[r], a_recv.at[r], at_z(toward(1)))

    def copy_b(r, j):
        return copy(part(sum1, r, j - 1), part(recv1, r, pair),
                    b_send.at[r, j - 1], b_recv.at[r, pair], at_z(toward(-j)))

    def from_b(r, i):
        p = lax.rem(pair + i, PAIRS)
        return copy(part(sum1, r, i - 1), part(recv1, r, p),
                    b_send.at[r, i - 1], b_recv.at[r, p], at_z(toward(-1)))

    def gateway(j):
        return toward(2) if j == 2 else toward(-j)

    def copy_c(r, j):
        to = gateway(j)
        return copy(part(send2, r, to // 2), part(got2, r, j - 1),
                    c_send.at[r, j - 1], c_recv.at[r, j - 1], at_z(to))

    def copy_d(r, j):
        owner = toward(-j)
        return copy(part(sum2, r, j), part(recv2, r, owner),
                    d_send.at[r, j], d_recv.at[r, owner], at_z(toward(1)))

    def from_d(r, k):
        owner = toward(k)
        return copy(part(sum2, r, k - 1), part(recv2, r, owner),
                    d_send.at[r, k - 1], d_recv.at[r, owner], at_z(toward(1)))

    def needs_c(j):
        return y + gateway(j) // 2 > 0

    def needs_d():
        return jnp.logical_or(y > 0, z != 1)

    def copy_y(r, i, arriving=False):
        o, n = lax.rem(y + i, NY), rows_of(r)
        s = lax.rem(y + NY - i, NY) if arriving else y
        return copy(ybuf.at[r, y, pl.ds(0, n)], ybuf.at[r, s, pl.ds(0, n)],
                    y_send.at[r, o], y_recv.at[r, s], y_peer(i))

    def head_from(i, arriving):
        return lax.rem(me + NH - i, NH) if arriving else me

    def copy_w(i, arriving=False):
        o, s = lax.rem(me + i, NH), head_from(i, arriving)
        return copy(w_ref.at[:, columns(o)], wbuf.at[s], w_send.at[o], w_recv.at[s], h_peer(i))

    def copy_n(h, i, arriving=False):
        s, held = head_from(2 * i, arriving), (ncat, early, last)[h]
        return copy(held.at[me], held.at[s], n_send.at[h, i], n_recv.at[h, s], h_peer(2 * i))

    sibling = {"head": me + 1 - 2 * lax.rem(me, 2)}

    def copy_pair(h, i, arriving=False):
        mine, held = lax.rem(me + NH - 2 * i, NH), (ncat, early, last)[h]
        s = mine + 1 - 2 * lax.rem(me, 2) if arriving else mine
        return copy(held.at[mine], held.at[s], p_send.at[h, i], n_recv.at[h, s], sibling)

    def each(count, do):
        def body(i, c):
            do(i)
            return c
        lax.fori_loop(1, count, body, 0)

    extra_state()
    for r in range(3):
        if r < 2:
            states(0, r)
        else:
            states(1, 0)
            states(1, 1)
        if r == 0:
            pl.semaphore_wait(barrier, NZ + NY + NH - 3)
        copy_a(r).start()
        if r == 2:
            copy_a(3).start()
    load(3).wait()
    each(NH, lambda i: copy_w(i).start())
    wbuf[me] = w_ref[:, columns(me)]

    load(2).wait()
    queries32 = q_ref[...].astype(F32) * 0.125
    prepare(queries32, qx, qz)
    for h in range(2):
        mine = low if h == 0 else jnp.logical_not(low)
        qf[h, 16] = jnp.where(mine, middle(queries32 * 2.0, qx), 0.0).astype(BF16)
        qf[h, 0] = products(qx, qz, h, 0, 1)[0]
        qz[h] = qz[h] * 2.0
        for i, feats in enumerate(products(qx, qz, h, 1, 15)):
            qf[h, i + 1] = feats

    def intra(h):
        mine = low if h == 0 else jnp.logical_not(low)
        masked = jnp.where(mine, queries32, 0.0).astype(BF16)
        for b in range(2):
            seen, first = 256 * (b + 1), 256 * b
            scores = nt(k_ref[0:seen, :], masked[first:first + 256])
            s_at = lax.broadcasted_iota(jnp.int32, (seen, 256), 0)
            t_at = lax.broadcasted_iota(jnp.int32, (seen, 256), 1) + first
            weights = jnp.where(s_at <= t_at, scores * scores, 0.0).astype(BF16)
            num[h, :, first:first + 256] = nn(vt[h * DH:(h + 1) * DH, 0:seen], weights)


    def combine(r):
        n = rows_of(r)
        copy_a(r).wait_recv()
        for j in (3, 2, 1):
            both = send1[r, NZ - j, 0:n, :].astype(F32) + got1[r, j, 0:n, :].astype(F32)
            sum1[r, j - 1, 0:n, :] = both.astype(BF16)
            copy_b(r, j).start()

    def totals(r):
        n = rows_of(r)
        both = send1[r, 0, 0:n, :].astype(F32) + got1[r, 0, 0:n, :].astype(F32)
        recv1[r, pair, 0:n, :] = both.astype(BF16)
        for i in range(1, PAIRS):
            from_b(r, i).wait_recv()
        total = recv1[r, 0, 0:n, :].astype(F32)
        for p in range(1, PAIRS):
            total += recv1[r, p, 0:n, :].astype(F32)
        ybuf[r, y, 0:n, :] = total.astype(BF16)

        def to_later(i):
            @pl.when(y + i < NY)
            def _():
                copy_y(r, i).start()
        each(NY, to_later)

    def prefixes(r):
        n = rows_of(r)

        def from_earlier(i):
            @pl.when(y >= i)
            def _():
                copy_y(r, i, True).wait_recv()
        each(NY, from_earlier)
        running = jnp.zeros((n, LANES), F32)
        for s in range(NY):
            running += jnp.where(s < y, ybuf[r, s, 0:n, :].astype(F32), 0.0)
        for p in range(PAIRS):
            send2[r, p, 0:n, :] = running.astype(BF16)
            running += recv1[r, p, 0:n, :].astype(F32)
        for j in (3, 2, 1):
            @pl.when(needs_c(j))
            def _(j=j):
                copy_c(r, j).start()
        share(r, 0, z, send2[r, pair, 0:n, :], send1[r, 0, 0:n, :], got1[r, 0, 0:n, :])

    def share(r, j, owner, before, mine, other):
        n = rows_of(r)
        after = (before.astype(F32) + jnp.where(even, mine, other).astype(F32)).astype(BF16)
        recv2[r, owner, 0:n, :] = jnp.where(even, before, after)
        sum2[r, j, 0:n, :] = jnp.where(even, after, before)

        @pl.when(needs_d())
        def _():
            copy_d(r, j).start()

    def relay(r):
        n = rows_of(r)

        @pl.when(y + pair == 0)
        def _():
            got2[r] = jnp.zeros(got2.shape[1:], BF16)

        for j in range(1, 4):
            @pl.when(y + pair > 0)
            def _(j=j):
                copy_c(r, j).wait_recv()
            share(r, j, toward(-j), got2[r, j - 1, 0:n, :], send1[r, NZ - j, 0:n, :], got1[r, j, 0:n, :])

    def arrived(r):
        @pl.when(y + z > 0)
        def _():
            for k in range(1, 5):
                from_d(r, k).wait_recv()

        @pl.when(y + z == 0)
        def _():
            recv2[r] = jnp.zeros(recv2.shape[1:], BF16)

    def read_out_first(half):
        arrived(half)
        prefix = [recv2[half, o, 0:DH, :] for o in range(NZ)]
        feats = [qf[0, half * NZ + o] for o in range(NZ)]
        if half == 0:
            pieces = [recv2[0, o, DH:DH + EXTRA, :].astype(F32)[:8] for o in range(NZ)]
            middles[...] = jnp.concatenate(pieces, axis=0).astype(BF16)
            prefix.append(middles[...])
            feats.append(qf[0, 16])
        num[0] += nt(jnp.concatenate(prefix, axis=1), jnp.concatenate(feats, axis=1))

    def read_out_second(r, owners, whole):
        first, n = (0, FIRST) if r == 2 else (FIRST, DH - FIRST)
        prefix = [recv2[r, o, half * n:(half + 1) * n, :] for half in range(2) for o in owners]
        feats = [qf[1, half * NZ + o] for half in range(2) for o in owners]
        if whole:
            prefix.append(middles[first:first + n, :])
            feats.append(qf[1, 16])
        num[1, first:first + n, :] += nt(jnp.concatenate(prefix, axis=1), jnp.concatenate(feats, axis=1))

    def read_out_near(r):
        read_out_second(r, [z] + [toward(-j) for j in range(1, 4)], True)

    def read_out_far(r):
        arrived(r)
        read_out_second(r, [toward(k) for k in range(1, 5)], False)

    load(4).wait()
    gains = jnp.transpose(jnp.broadcast_to(gain_ref[...], (LANES, LANES)))

    def gain_of(first, n):
        return jnp.concatenate([gains[first:first + n]] * (tok // LANES), axis=1)

    def inverse_norm(h):
        value = num[h]
        return lax.rsqrt(jnp.mean(value * value, axis=0, keepdims=True) + EPSILON)

    def spread(h):
        for i in (2, 1, 3):
            copy_n(h, i).start()
        copy_pair(h, 0).start()

    def give_first():
        ncat[me] = (num[0] * inverse_norm(0) * gain_of(0, DH)).astype(BF16)
        spread(0)

    def give_early():
        early[me] = (num[1, 0:FIRST, :] * gain_of(DH, FIRST)).astype(BF16)
        spread(1)

    def give_last():
        n = DH - FIRST
        last[me, :, 0:tok] = (num[1, FIRST:DH, :] * gain_of(DH + FIRST, n)).astype(BF16)
        flat = inverse_norm(1)
        scale = jnp.concatenate([flat[:, i * LANES:(i + 1) * LANES] for i in range(tok // LANES)], axis=0)
        high = scale.astype(BF16).astype(F32)
        side = jnp.concatenate([high, scale - high, jnp.zeros((n - 8, LANES), F32)], axis=0)
        last[me, :, tok:tok + LANES] = side.astype(BF16)
        spread(2)

    def pass_on(h):
        for i in (1, 3, 2):
            copy_n(h, i, True).wait_recv()
            copy_pair(h, i).start()

    def gathered(h):
        for i in range(NH // 2):
            copy_pair(h, i, True).wait_recv()

    def project_second(s):
        block = jnp.concatenate([early[s], last[s, :, 0:tok]], axis=0)
        side = last[s, :, tok:tok + LANES].astype(F32)
        parts = tok // LANES
        scale = side[0:parts] + side[parts:2 * parts]
        flat = jnp.concatenate([scale[i:i + 1] for i in range(parts)], axis=1)
        acc[...] += nn(wt2[s], block) * flat

    combine(0)
    intra(0)
    combine(1)
    intra(1)
    combine(2)
    combine(3)
    each(NH, lambda i: copy_w(i, True).wait_recv())
    turned = [jnp.transpose(wbuf[s].astype(F32)) for s in range(NH)]
    wt[...] = jnp.concatenate([t[:, 0:DH] for t in turned], axis=1).astype(BF16)
    for s in range(NH):
        wt2[s] = turned[s][:, DH:].astype(BF16)
    for r in range(ROUNDS):
        totals(r)
    for r in range(ROUNDS):
        prefixes(r)
    for r in range(ROUNDS):
        relay(r)
    read_out_first(0)
    read_out_first(1)
    give_first()
    read_out_near(2)
    read_out_near(3)
    read_out_far(2)
    give_early()
    read_out_far(3)
    give_last()
    pass_on(0)
    gathered(0)
    acc[...] = nn(wt[...], jnp.concatenate([ncat[s] for s in range(NH)], axis=0))
    pass_on(1)
    pass_on(2)
    gathered(1)
    project_second(me)
    for i in range(1, NH // 2):
        project_second(lax.rem(me + 2 * i, NH))
    for i in range(NH // 2):
        copy_pair(2, i, True).wait_recv()
        project_second(lax.rem(me + NH - 2 * i, NH) + 1 - 2 * lax.rem(me, 2))
    out_ref[...] = jnp.transpose(acc[...]).astype(BF16)

    for r in range(ROUNDS):
        copy_a(r).wait_send()

        def sent(i, r=r):
            @pl.when(y + i < NY)
            def _():
                copy_y(r, i).wait_send()
        each(NY, sent)
        for j in range(1, 4):
            copy_b(r, j).wait_send()

            @pl.when(needs_c(j))
            def _(r=r, j=j):
                copy_c(r, j).wait_send()

        @pl.when(needs_d())
        def _(r=r):
            for j in range(4):
                copy_d(r, j).wait_send()
    each(NH, lambda i: copy_w(i).wait_send())
    for h in range(3):
        each(NH // 2, lambda i: copy_n(h, i).wait_send())
        for i in range(NH // 2):
            copy_pair(h, i).wait_send()


def per_device(queries, keys, values, gain, out_weight):
    tok, width = queries.shape
    rows = max(ROWS)
    vmem = pl.BlockSpec(memory_space=pltpu.VMEM)
    dma = pltpu.SemaphoreType.DMA
    return pl.pallas_call(
        kernel,
        out_shape=jax.ShapeDtypeStruct((tok, width), BF16),
        in_specs=[pl.BlockSpec(memory_space=pltpu.HBM)] * 5,
        out_specs=vmem,
        scratch_shapes=[
            pltpu.VMEM((tok, width), BF16),
            pltpu.VMEM((tok, width), BF16),
            pltpu.VMEM((tok, width), BF16),
            pltpu.VMEM((1, width), F32),
            pltpu.VMEM(out_weight.shape, BF16),
            pltpu.VMEM((2, tok, LANES), F32),
            pltpu.VMEM((2, tok, LANES), F32),
            pltpu.VMEM((2, tok, LANES), F32),
            pltpu.VMEM((2, tok, LANES), F32),
            pltpu.VMEM((LANES, tok), BF16),
            pltpu.VMEM((2, 17, tok, LANES), BF16),
            pltpu.VMEM((2, DH, tok), F32),
            pltpu.VMEM((NH, LANES, LANES), BF16),
            pltpu.VMEM((LANES, NH * DH), BF16),
            pltpu.VMEM((NH, LANES, DH), BF16),
            pltpu.VMEM((LANES, tok), F32),
            pltpu.VMEM((DH, LANES), BF16),
            pltpu.VMEM((NH, DH, tok), BF16),
            pltpu.VMEM((NH, FIRST, tok), BF16),
            pltpu.VMEM((NH, DH - FIRST, tok + LANES), BF16),
            pltpu.VMEM((ROUNDS, NZ, rows, LANES), BF16),
            pltpu.VMEM((ROUNDS, 4, rows, LANES), BF16),
            pltpu.VMEM((ROUNDS, 3, rows, LANES), BF16),
            pltpu.VMEM((ROUNDS, PAIRS, rows, LANES), BF16),
            pltpu.VMEM((ROUNDS, NY, rows, LANES), BF16),
            pltpu.VMEM((ROUNDS, PAIRS, rows, LANES), BF16),
            pltpu.VMEM((ROUNDS, 3, rows, LANES), BF16),
            pltpu.VMEM((ROUNDS, 4, rows, LANES), BF16),
            pltpu.VMEM((ROUNDS, NZ, rows, LANES), BF16),
            dma((ROUNDS,)), dma((ROUNDS,)),
            dma((ROUNDS, 3)), dma((ROUNDS, PAIRS)),
            dma((ROUNDS, NY)), dma((ROUNDS, NY)),
            dma((ROUNDS, 3)), dma((ROUNDS, 3)),
            dma((ROUNDS, 4)), dma((ROUNDS, NZ)),
            dma((NH,)), dma((NH,)),
            dma((3, NH // 2)), dma((3, NH)), dma((3, NH // 2)),
            dma((5,)),
        ],
        compiler_params=pltpu.CompilerParams(
            collective_id=0, has_side_effects=True, vmem_limit_bytes=55040 << 10),
    )(queries, keys, values, gain.reshape(1, width), out_weight)


def solution(mesh):
    return jax.shard_map(
        per_device,
        mesh=mesh,
        in_specs=(P("ctx", "head"), P("ctx", "head"), P("ctx", "head"), P("head"), P("head", None)),
        out_specs=P("ctx", "head"),
        check_vma=False,
    )
```
